32 devices in a mesh: grp: 2 (over y), ex: 8 (over z, x), tp: 2 (over core).
Axes of the slice: x: 2, y: 2, z: 4, core: 2. Of those that a mesh axis runs over, the one named last changes fastest.
Arguments:
- hidden_states: bfloat16 [64, 3584], P(('grp', 'ex')), parts along dimension 0
- draft_row: int32 [64], P(('grp', 'ex')), parts along dimension 0, may hold values from 0 to 31, as said below
- expert_ids: int32 [2, 64, 8], P(None, ('grp', 'ex')), parts along dimension 1, may hold values from 0 to 7, all different within a row; in each aligned block of 4 rows (0 to 3, 4 to 7, ..., all dimensions but the last counted through in order) at most 4 rows name the same one
- route_weights: float32 [2, 64, 8], P(None, ('grp', 'ex')), parts along dimension 1, may hold values from 0.1 to 0.6
- norm_gain: float32 [3584], replicated, may hold values from 0.1 to 1.9
- w_gate: bfloat16 [3584, 8192], P(None, ('ex', 'tp')), may hold values from -0.09375 to 0.09375
- w_up: bfloat16 [3584, 8192], P(None, ('ex', 'tp')), may hold values from -0.09375 to 0.09375
- w_down: bfloat16 [8192, 3584], P(('ex', 'tp')), may hold values from -0.1875 to 0.1875
Outputs:
- draft_hidden: bfloat16 [64, 3584], P(('grp', 'ex')), parts along dimension 0
The draws below stay inside these ranges and needn't reach their ends.
There are 2 independent parts, one for each index of `grp`. The reference program is written for one: setup_inputs(seed, part) draws one part's arguments, and reference() takes and returns one part's arrays. A program takes and returns all parts, laid end to end along the dimension named above; an argument that names none is the same for every part. Nothing has to cross between parts.
Inputs may be any that keep to these rules, and one draw needn't show every extreme that they name: draft_row is a permutation of the 32 rows; draft row r lies on index r // 4 of ex; the 4 decode rows of one index go to at most 2 rows of any one draft index, and some pairs reach 2. `expert_ids`: each row names 8 different experts; of the 4 rows of one index of ex in one step, at most 4 name the same expert, and some expert reaches 4.
All inputs are finite; a program needn't handle non-finite values.
Results may differ from the reference program's by a relative error of at most 0.019.
Values may be sent and summed in bfloat16 or wider, within the bound.
A program may use at most 64 MiB of HBM per device.

```python
import math
import jax
import jax.numpy as jnp
import numpy as np
from jax import lax

D = 3584
HID = 1024
TOP = 8
STEPS = 2
RCAP = 2
ROW_DEV = 4
ROWS = 32
EXPERTS = 8
CAP = 4
N_EX = 8


def draw_hidden_states(key, part):
    key = jax.random.fold_in(key, 5)
    key_base, key_cols, key_rows = jax.random.split(key, 3)
    col_scale = jnp.exp((jax.random.uniform(key_cols, (1, D), jnp.float32) - 0.5) * math.log(10.0))
    row_scale = jnp.exp((jax.random.uniform(key_rows, (ROWS, 1), jnp.float32) - 0.5) * math.log(10.0))
    base = jax.random.truncated_normal(key_base, -4.0, 4.0, (ROWS, D), jnp.float32)
    return (0.5 * base * col_scale * row_scale).astype(jnp.bfloat16)


def draw_draft_row(key, part):
    key = jax.random.fold_in(key, 11)
    key_outer, key_inner, key_rows = jax.random.split(key, 3)
    device_count = ROWS // ROW_DEV
    outer_perm = jax.random.permutation(key_outer, device_count)
    inner_perm = jax.random.permutation(key_inner, device_count)
    devices = jnp.arange(device_count, dtype=jnp.int32)
    slot_ids = jnp.arange(ROW_DEV, dtype=jnp.int32)
    block_ids = slot_ids // RCAP
    source_dev = outer_perm[(inner_perm[devices][:, None] + block_ids[None, :]) % device_count]
    row_perms = jax.vmap(lambda sub_key: jax.random.permutation(sub_key, ROW_DEV))(jax.random.split(key_rows, device_count))
    source_row = source_dev * ROW_DEV + row_perms[source_dev, slot_ids[None, :]]
    targets = jnp.arange(ROWS, dtype=jnp.int32)
    return jnp.zeros((ROWS,), jnp.int32).at[source_row.reshape(-1)].set(targets)


def steps_of(own_key, dims, pieces, low, top_value):
    def one(dim, blocks):
        draws = jax.random.uniform(jax.random.fold_in(jax.random.fold_in(own_key, 6), dim), (blocks,), jnp.float32, low / len(pieces), top_value / len(pieces))
        return jnp.repeat(jnp.exp(draws), dims[dim] // blocks).reshape((-1,) + (1,) * (len(dims) - dim - 1))

    loudness = one(*pieces[0])
    for cut in pieces[1:]:
        loudness = loudness * one(*cut)
    return loudness


def deal_out(key, own, number, rows, amount, top, most, slope):
    order = jax.random.permutation(key, amount)
    crowded, usual = shares(amount, rows * top, most, slope, True), shares(amount, rows * top, most, slope, False)
    places = jnp.arange(amount)

    def named(sizes, rotation):
        used = int((sizes > 0).sum())
        fixed = max(1, used // 4)
        passed = fixed + (places - fixed + rotation * (used - fixed)) % max(1, amount - fixed)
        return jnp.zeros((amount,), jnp.int32).at[order[jnp.where(places < fixed, places, passed)]].set(jnp.asarray(sizes, jnp.int32))

    sizes = jnp.where(number % 4 == 0, named(crowded, number // 4), named(usual, number - number // 4 - 1))
    mixed = jax.random.permutation(jax.random.fold_in(own, 3), amount)
    source_of, sink = mixed[0:amount // 2 * 2:2], mixed[1:amount // 2 * 2:2]
    room = jnp.minimum(sizes[source_of] - 1, most - sizes[sink]) // 2
    room = jnp.where((source_of == order[0]) | (sink == order[0]) | (sizes[sink] == 0), 0, jnp.maximum(room, 0))
    passed = jax.random.randint(jax.random.fold_in(own, 4), (amount // 2,), 0, 1 << 20) % (room + 1)
    sizes = sizes.at[source_of].add(-passed).at[sink].add(passed)
    items = jnp.searchsorted(jnp.cumsum(sizes), jnp.arange(rows * top), side="right").astype(jnp.int32)
    table = items.reshape(top, rows).T
    table = table[jax.random.permutation(jax.random.fold_in(own, 1), rows)]
    rotation = jax.random.randint(jax.random.fold_in(own, 2), (rows, 1), 0, top)
    return jnp.take_along_axis(table, (jnp.arange(top)[None, :] + rotation) % top, axis=1)


def shares(amount, total, bound, skew, full):
    weights = [(1 << 20) // math.isqrt(rank ** skew) + 1 for rank in range(1, amount + 1)]
    largest = bound if full else min(bound, max(-(-total // amount), total * weights[0] // sum(weights)))
    least = 1 if total - largest >= amount - 1 else 0
    holding, spare = [largest] + [least] * (amount - 1), total - largest - least * (amount - 1)
    while spare > 0:
        free = [i for i in range(1, amount) if holding[i] < largest] or [i for i in range(1, amount) if holding[i] < bound]
        whole, remaining = sum([weights[i] for i in free]), spare
        for i in free:
            more = min(bound - holding[i], max(1, remaining * weights[i] // whole), spare)
            holding[i] = holding[i] + more
            spare = spare - more
    return np.array(holding)


def gaussian(key, dims, scale, reach, shards=(), held_as=jnp.bfloat16):
    drawn = scale * jax.random.normal(key, dims, jnp.float32)
    if shards:
        drawn = drawn * steps_of(key, dims, shards, -0.22, 0.18)
    return jnp.clip(drawn, -reach, reach).astype(held_as)


def setup_inputs(seed: int = 0, part: int = 0) -> dict:
    seeds = jax.random.split(jax.random.key(seed), 9)
    part_keys = jax.random.split(jax.random.fold_in(seeds[8], part), 9)
    hidden_states = draw_hidden_states(jax.random.fold_in(jax.random.fold_in(seeds[8], part), 71), part)
    draft_row = draw_draft_row(jax.random.fold_in(jax.random.fold_in(seeds[8], part), 71), part)
    expert_ids_keys = jax.random.split(jax.random.fold_in(part_keys[2], 1), STEPS * ROWS // ROW_DEV)
    expert_ids_turns = jax.random.permutation(jax.random.fold_in(part_keys[2], 3), STEPS * ROWS // ROW_DEV)
    expert_ids = jax.vmap(lambda own, number: deal_out(jax.random.fold_in(part_keys[2], 2), own, number, ROW_DEV, EXPERTS, TOP, CAP, 2))(expert_ids_keys, expert_ids_turns).reshape((STEPS, ROWS, TOP))
    route_weights = jnp.clip(0.1 + 0.5 * jax.random.uniform(part_keys[3], (STEPS, ROWS, TOP), jnp.float32) ** steps_of(part_keys[3], (STEPS, ROWS, TOP), ((1, 8),), -0.2, 0.2), 0.1, 0.6)
    norm_gain = jnp.clip(1.0 + 0.18 * jax.random.normal(seeds[4], (D,), jnp.float32), 0.1, 1.9)
    w_gate = gaussian(seeds[5], (D, EXPERTS * HID), D ** -0.5, 0.09375, ((1, 16),))
    w_up = gaussian(seeds[6], (D, EXPERTS * HID), D ** -0.5, 0.09375, ((1, 16),))
    w_down = gaussian(seeds[7], (EXPERTS * HID, D), HID ** -0.5, 0.1875, ((0, 16),))
    return {"hidden_states": hidden_states, "draft_row": draft_row, "expert_ids": expert_ids, "route_weights": route_weights, "norm_gain": norm_gain, "w_gate": w_gate, "w_up": w_up, "w_down": w_down}


def rms_norm(values, norm_gain):
    as_float = values.astype(jnp.float32)
    mean_square = lax.optimization_barrier(jnp.mean(as_float * as_float, axis=-1, keepdims=True))
    return (as_float * lax.rsqrt(mean_square + 1e-06) * norm_gain).astype(jnp.bfloat16)

def reference(hidden_states, draft_row, expert_ids, route_weights, norm_gain, w_gate, w_up, w_down):
    current = jnp.zeros_like(hidden_states).at[draft_row].set(hidden_states)
    capacity = CAP * N_EX
    for step_no in range(STEPS):
        normed = rms_norm(current, norm_gain)
        step_ids = expert_ids[step_no]
        weights = route_weights[step_no]

        def add_expert(running, expert):
            matches = step_ids == expert
            chosen = jnp.any(matches, axis=1)
            route_coef = lax.optimization_barrier(jnp.sum(jnp.where(matches, weights, 0.0), axis=1))
            ordering = jnp.argsort(jnp.where(chosen, 0, 1).astype(jnp.int32), stable=True)[:capacity]
            picked = normed[ordering]
            offset = expert * HID
            gate_cols = lax.dynamic_slice_in_dim(w_gate, offset, HID, 1)
            up_cols = lax.dynamic_slice_in_dim(w_up, offset, HID, 1)
            down_rows = lax.dynamic_slice_in_dim(w_down, offset, HID, 0)
            gate_proj = jnp.dot(picked, gate_cols, preferred_element_type=jnp.float32)
            up_proj = jnp.dot(picked, up_cols, preferred_element_type=jnp.float32)
            activated = (jax.nn.silu(gate_proj) * up_proj).astype(jnp.bfloat16)
            expert_out = jnp.dot(activated, down_rows, preferred_element_type=jnp.float32)
            return (running.at[ordering].add(expert_out * route_coef[ordering][:, None]), None)
        moe, _ = lax.scan(add_expert, jnp.zeros(hidden_states.shape, jnp.float32), jnp.arange(EXPERTS, dtype=jnp.int32))
        current = (current.astype(jnp.float32) + moe).astype(jnp.bfloat16)
    return current
```

```python
import functools

import jax
import jax.numpy as jnp
from jax import lax
from jax.experimental import pallas as pl
from jax.experimental.pallas import tpu as pltpu
from jax.sharding import PartitionSpec as P

HID = 1024
STEPS = 2
RCAP = 2


epsilon = 1e-06


def expert_block(rows_in, w_gate, w_up, w_down):
    gate_proj = jnp.dot(rows_in, w_gate, preferred_element_type=jnp.float32)
    up_proj = jnp.dot(rows_in, w_up, preferred_element_type=jnp.float32)
    activated = (jax.nn.silu(gate_proj) * up_proj).astype(jnp.bfloat16)
    return jnp.dot(activated, w_down, preferred_element_type=jnp.float32)


def fold_back(returned, seating, route_coef, experts, group_size):
    ex_size, slot_cap, columns = returned.shape
    summed = returned.reshape(experts, group_size, slot_cap, columns).sum(axis=1)
    scale = seating.astype(jnp.float32) * route_coef.T[:, None, :]
    return jnp.einsum(
        "ecr,ecd->rd",
        scale,
        summed,
        precision=lax.Precision.HIGHEST,
        preferred_element_type=jnp.float32,
    )


def shards(hidden_states, draft_row, expert_ids, route_weights, norm_gain, w_gate, w_up, w_down):
    row_dev, features = hidden_states.shape
    ex_size = lax.axis_size("ex")
    tp_size = lax.axis_size("tp")
    hid_dev = w_gate.shape[1]
    group_size = HID // (hid_dev * tp_size)
    experts = ex_size // group_size
    chosen_count = expert_ids.shape[2]
    slot_cap = min(row_dev, max(2, 2 * row_dev * chosen_count // experts))
    target_dev = draft_row // row_dev
    target_pos = draft_row % row_dev
    same_dest = target_dev[:, None] == target_dev[None, :]
    earlier = jnp.tril(jnp.ones((row_dev, row_dev), jnp.bool_), -1)
    order_in = jnp.sum(same_dest & earlier, axis=1)
    slot_index = target_dev * RCAP + order_in
    picker = jnp.arange(ex_size * RCAP, dtype=jnp.int32)[:, None] == slot_index[None, :]
    outgoing = (
        jnp.dot(picker.astype(jnp.bfloat16), hidden_states, preferred_element_type=jnp.float32)
        .astype(jnp.bfloat16)
        .reshape(ex_size, RCAP, features)
    )
    labels = (
        jnp.sum(jnp.where(picker, target_pos[None, :] + 1, 0), axis=1)
        .astype(jnp.bfloat16)
        .reshape(ex_size, RCAP)
    )
    arrived, arrived_labels = (
        lax.all_to_all(outgoing, "ex", split_axis=0, concat_axis=0, tiled=True),
        lax.all_to_all(labels, "ex", split_axis=0, concat_axis=0, tiled=True),
    )
    arrived = arrived.reshape(ex_size * RCAP, features)
    settle = (
        arrived_labels.reshape(-1).astype(jnp.float32)[None, :]
        == (jnp.arange(row_dev) + 1).astype(jnp.float32)[:, None]
    )
    current = jnp.dot(
        settle.astype(jnp.bfloat16), arrived, preferred_element_type=jnp.float32
    ).astype(jnp.bfloat16)
    slot_total = ex_size * slot_cap
    for step_no in range(STEPS):
        as_float = current.astype(jnp.float32)
        mean_square = jnp.mean(as_float * as_float, axis=-1, keepdims=True)
        normed = (as_float * lax.rsqrt(mean_square + epsilon) * norm_gain).astype(jnp.bfloat16)
        step_ids = expert_ids[step_no]
        weights = route_weights[step_no]
        matches = step_ids[:, :, None] == jnp.arange(experts, dtype=jnp.int32)[None, None, :]
        chosen = jnp.any(matches, axis=1)
        route_coef = jnp.sum(jnp.where(matches, weights[:, :, None], 0.0), axis=1)
        chosen_int = chosen.astype(jnp.int32)
        before = jnp.cumsum(chosen_int, axis=0) - chosen_int
        seating = chosen.T[:, None, :] & (
            before.T[:, None, :] == jnp.arange(slot_cap, dtype=jnp.int32)[None, :, None]
        )
        packed_base = jnp.einsum(
            "ecr,rd->ecd", seating.astype(jnp.bfloat16), normed, preferred_element_type=jnp.float32
        ).astype(jnp.bfloat16)
        occupancy = jnp.any(seating, axis=2).astype(jnp.bfloat16)
        occupancy = jnp.broadcast_to(occupancy[:, None], (experts, group_size, slot_cap)).reshape(
            ex_size, slot_cap
        )
        packed = jnp.broadcast_to(
            packed_base[:, None], (experts, group_size, slot_cap, features)
        ).reshape(ex_size, slot_cap, features)
        landed, landed_flags = (
            lax.all_to_all(packed, "ex", split_axis=0, concat_axis=0, tiled=True),
            lax.all_to_all(occupancy, "ex", split_axis=0, concat_axis=0, tiled=True),
        )
        rows_in = landed.reshape(slot_total, features)
        partial_value = expert_block(rows_in, w_gate, w_up, w_down)
        returned = lax.all_to_all(
            partial_value.reshape(ex_size, slot_cap, features).astype(jnp.bfloat16),
            "ex",
            split_axis=0,
            concat_axis=0,
            tiled=True,
        ).astype(jnp.float32)
        branch_sum = lax.psum(
            fold_back(returned, seating, route_coef, experts, group_size).astype(jnp.bfloat16), "tp"
        ).astype(jnp.float32)
        current = (current.astype(jnp.float32) + branch_sum).astype(jnp.bfloat16)
    return current


QUARTERS = 4
PIECE = 512
MESH = pl.DeviceIdType.MESH


def one_hot(condition, dtype=jnp.bfloat16):
    return jnp.where(condition, 1.0, 0.0).astype(dtype)


def fused_kernel(
    n,
    hidden_ref,
    place_ref,
    ids_ref,
    weights_ref,
    gain_ref,
    wg_hbm,
    wu_hbm,
    wd_hbm,
    out_ref,
    wg,
    wu,
    wd,
    first,
    second,
    normed,
    swap_out,
    swap_in,
    stage,
    parts_out,
    parts_in,
    coef,
    last,
    weight_sem,
    gather_send,
    gather_recv,
    pass_send,
    pass_recv,
    swap_send,
    swap_recv,
    back_send,
    back_recv,
    last_send,
    last_recv,
):
    rows, features = hidden_ref.shape
    half = features // 2
    block = QUARTERS * rows
    total = n * rows
    widths = [min(PIECE, half - q * PIECE) for q in range(QUARTERS)]
    grp, me, core = lax.axis_index("grp"), lax.axis_index("ex"), lax.axis_index("tp")
    other = 1 - core

    weight_copies = []
    for h in range(2):
        span = pl.ds(h * half, half)
        for which, (source, target) in enumerate(
            (
                (wg_hbm.at[span, :], wg.at[span, :]),
                (wu_hbm.at[span, :], wu.at[span, :]),
                (wd_hbm.at[:, span], wd.at[h]),
            )
        ):
            weight_copies.append(
                (which, pltpu.make_async_copy(source, target, weight_sem.at[h * 3 + which]))
            )
    for which, copy in sorted(weight_copies, key=lambda pair: pair[0]):
        copy.start()

    barrier = pltpu.get_barrier_semaphore()
    for off in range(1, n):
        pl.semaphore_signal(
            barrier, inc=1, device_id=(grp, lax.rem(me + off, n), core), device_id_type=MESH
        )
    pl.semaphore_signal(barrier, inc=1, device_id=(grp, me, other), device_id_type=MESH)

    mine = pl.ds(pl.multiple_of(me * block, block), block)
    stage[...] = jnp.zeros_like(stage)
    held = hidden_ref[...].astype(jnp.float32)
    for h in range(2):
        for q in range(QUARTERS):
            start = h * half + q * PIECE
            stage[pl.ds(h * block + q * rows, rows), pl.ds(0, widths[q])] = held[
                :, start : start + widths[q]
            ]
    line = lax.broadcasted_iota(jnp.int32, (block, QUARTERS * total), 0)
    lane = lax.broadcasted_iota(jnp.int32, (block, QUARTERS * total), 1)
    place = jnp.zeros_like(line)
    for r in range(rows):
        place = jnp.where(line % rows == r, place_ref[r], place)
    placing = one_hot((line // rows == lane // total) & (lane % total == place))
    for h in range(2):
        first[h, mine, pl.ds(0, PIECE)] = stage[pl.ds(h * block, block), :].astype(jnp.bfloat16)
        first[h, mine, pl.ds(PIECE, QUARTERS * total)] = placing

    pl.semaphore_wait(barrier, n)

    def gather_start(step, buf):
        sends = []
        for off in range(1, n):
            copy = pltpu.make_async_remote_copy(
                src_ref=buf.at[core, mine, :],
                dst_ref=buf.at[core, mine, :],
                send_sem=gather_send.at[step, off],
                recv_sem=gather_recv.at[step, off],
                device_id=(grp, lax.rem(me + off, n), core),
                device_id_type=MESH,
            )
            copy.start()
            sends.append(copy)
        return sends

    def pass_on(step, buf, off):
        slot = pl.ds(pl.multiple_of(lax.rem(me + n - off, n) * block, block), block)
        copy = pltpu.make_async_remote_copy(
            src_ref=buf.at[core, slot, :],
            dst_ref=buf.at[core, slot, :],
            send_sem=pass_send.at[step, off],
            recv_sem=pass_recv.at[step, off],
            device_id=(grp, me, other),
            device_id_type=MESH,
        )
        copy.start()
        return copy

    pending = []
    sends = gather_start(0, first)
    pending += sends

    for step in range(STEPS):
        ids = ids_ref[step]
        weights = weights_ref[step]
        for e in range(n):
            value = jnp.sum(jnp.where(ids == e, weights, 0.0), axis=1, keepdims=True)
            value = jnp.broadcast_to(value, (rows, 128))
            for q in range(QUARTERS):
                coef[step, e, pl.ds(q * rows, rows), :] = value
    stage[...] = jnp.zeros_like(stage)

    current = None
    for step in range(STEPS):
        buf = first if step == 0 else second
        passes = []
        if step > 0:
            passes.append(pass_on(step, buf, 0))
        for off in range(1, n):
            sends[off - 1].wait_recv()
            passes.append(pass_on(step, buf, off))
        for copy in passes:
            copy.wait_recv()
        pending += passes

        if step == 0:
            pick = jnp.transpose(first[0, :, pl.ds(PIECE, QUARTERS * total)].astype(jnp.float32))
            pick = pick.astype(jnp.bfloat16)
        else:
            to = lax.broadcasted_iota(jnp.int32, (QUARTERS * total, n * block), 0)
            at = lax.broadcasted_iota(jnp.int32, (QUARTERS * total, n * block), 1)
            pick = one_hot(
                (to // total == (at // rows) % QUARTERS)
                & (to % total == (at // block) * rows + at % rows)
            )
        spread = [
            jnp.dot(pick, buf[h, :, pl.ds(0, PIECE)], preferred_element_type=jnp.float32)
            for h in range(2)
        ]
        squares = jnp.sum(spread[0] * spread[0] + spread[1] * spread[1], axis=1, keepdims=True)
        square = squares[0:total]
        for q in range(1, QUARTERS):
            square = square + squares[q * total : (q + 1) * total]
        scale = lax.rsqrt(square / features + epsilon)
        for h in range(2):
            for q in range(QUARTERS):
                start = h * half + q * PIECE
                piece = spread[h][q * total : (q + 1) * total, : widths[q]]
                gain = gain_ref[:, pl.ds(start, widths[q])]
                normed[:, pl.ds(start, widths[q])] = (piece * scale * gain).astype(jnp.bfloat16)
        if step == 0:
            for which, copy in weight_copies:
                if which < 2:
                    copy.wait()
        gate = jnp.dot(normed[...], wg[...], preferred_element_type=jnp.float32)
        up = jnp.dot(normed[...], wu[...], preferred_element_type=jnp.float32)
        act = (gate / (1.0 + jnp.exp(-gate)) * up).astype(jnp.bfloat16)
        if step == 0:
            for which, copy in weight_copies:
                if which == 2:
                    copy.wait()
        for q in range(QUARTERS):
            cols = pl.ds(q * PIECE, widths[q])
            swap_out[step, :, cols] = jnp.dot(
                act, wd[other, :, cols], preferred_element_type=jnp.float32
            ).astype(jnp.bfloat16)
        swap = pltpu.make_async_remote_copy(
            src_ref=swap_out.at[step],
            dst_ref=swap_in.at[step],
            send_sem=swap_send.at[step],
            recv_sem=swap_recv.at[step],
            device_id=(grp, me, other),
            device_id_type=MESH,
        )
        swap.start()
        own = [
            jnp.dot(
                act, wd[core, :, pl.ds(q * PIECE, widths[q])], preferred_element_type=jnp.float32
            )
            for q in range(QUARTERS)
        ]
        if step == 0:
            to = lax.broadcasted_iota(jnp.int32, (block, QUARTERS * total), 0)
            at = lax.broadcasted_iota(jnp.int32, (block, QUARTERS * total), 1)
            keep = one_hot((to // rows == at // total) & (at % total == me * rows + to % rows))
            spread_own = jnp.where(core == 0, spread[0], spread[1]).astype(jnp.bfloat16)
            current = jnp.dot(keep, spread_own, preferred_element_type=jnp.float32)
        swap.wait_recv()
        pending.append(swap)
        for q in range(QUARTERS):
            cols = pl.ds(q * PIECE, widths[q])
            value = own[q] + swap_in[step, :, cols].astype(jnp.float32)
            for p in range(n):
                stage[pl.ds(p * block + q * rows, rows), pl.ds(0, widths[q])] = value[
                    p * rows : (p + 1) * rows
                ]
        parts_out[step] = stage[...].astype(jnp.bfloat16)
        backs = []
        for off in range(1, n):
            peer = lax.rem(me + off, n)
            copy = pltpu.make_async_remote_copy(
                src_ref=parts_out.at[step, pl.ds(pl.multiple_of(peer * block, block), block), :],
                dst_ref=parts_in.at[step, mine, :],
                send_sem=back_send.at[step, off],
                recv_sem=back_recv.at[step, off],
                device_id=(grp, peer, core),
                device_id_type=MESH,
            )
            copy.start()
            backs.append(copy)
        parts_in[step, mine, :] = parts_out[step, mine, :]
        for copy in backs:
            copy.wait_recv()
        pending += backs
        moe = None
        for e in range(n):
            value = parts_in[step, pl.ds(e * block, block), :].astype(jnp.float32)
            value = value * jnp.concatenate([coef[step, e]] * (PIECE // 128), axis=1)
            moe = value if moe is None else moe + value
        result = (current + moe).astype(jnp.bfloat16)
        current = result.astype(jnp.float32)
        if step < STEPS - 1:
            second[core, mine, :] = result
            sends = gather_start(step + 1, second)
            pending += sends

    last[core] = result
    final = pltpu.make_async_remote_copy(
        src_ref=last.at[core],
        dst_ref=last.at[core],
        send_sem=last_send,
        recv_sem=last_recv,
        device_id=(grp, me, other),
        device_id_type=MESH,
    )
    final.start()
    final.wait_recv()
    pending.append(final)
    for h in range(2):
        value = last[h].astype(jnp.float32)
        for q in range(QUARTERS):
            out_ref[:, pl.ds(h * half + q * PIECE, widths[q])] = value[
                q * rows : (q + 1) * rows, : widths[q]
            ].astype(jnp.bfloat16)
    for copy in pending:
        copy.wait_send()


def fused_shards(hidden_states, draft_row, expert_ids, route_weights, norm_gain, w_gate, w_up, w_down):
    rows, features = hidden_states.shape
    hid_dev = w_gate.shape[1]
    n = lax.axis_size("ex")
    block = QUARTERS * rows
    half = features // 2
    spread = QUARTERS * n * rows
    vmem, any_space = pl.BlockSpec(memory_space=pltpu.VMEM), pl.BlockSpec(memory_space=pl.ANY)
    dma = pltpu.SemaphoreType.DMA
    return pl.pallas_call(
        functools.partial(fused_kernel, n),
        out_shape=jax.ShapeDtypeStruct((rows, features), jnp.bfloat16),
        in_specs=[vmem, pl.BlockSpec(memory_space=pltpu.SMEM), vmem, vmem, vmem]
        + [any_space] * 3,
        out_specs=vmem,
        scratch_shapes=[
            pltpu.VMEM((features, hid_dev), jnp.bfloat16),
            pltpu.VMEM((features, hid_dev), jnp.bfloat16),
            pltpu.VMEM((2, hid_dev, half), jnp.bfloat16),
            pltpu.VMEM((2, n * block, PIECE + spread), jnp.bfloat16),
            pltpu.VMEM((2, n * block, PIECE), jnp.bfloat16),
            pltpu.VMEM((n * rows, features), jnp.bfloat16),
            pltpu.VMEM((STEPS, n * rows, half), jnp.bfloat16),
            pltpu.VMEM((STEPS, n * rows, half), jnp.bfloat16),
            pltpu.VMEM((n * block, PIECE), jnp.float32),
            pltpu.VMEM((STEPS, n * block, PIECE), jnp.bfloat16),
            pltpu.VMEM((STEPS, n * block, PIECE), jnp.bfloat16),
            pltpu.VMEM((STEPS, n, block, 128), jnp.float32),
            pltpu.VMEM((2, block, PIECE), jnp.bfloat16),
            dma((6,)),
            dma((STEPS, n)),
            dma((STEPS, n)),
            dma((STEPS, n)),
            dma((STEPS, n)),
            dma((STEPS,)),
            dma((STEPS,)),
            dma((STEPS, n)),
            dma((STEPS, n)),
            dma,
            dma,
        ],
        compiler_params=pltpu.CompilerParams(
            collective_id=0, has_side_effects=True, vmem_limit_bytes=48 * 1024 * 1024
        ),
        cost_estimate=pl.CostEstimate(
            flops=STEPS * 6 * n * rows * features * hid_dev,
            bytes_accessed=6 * features * hid_dev,
            transcendentals=STEPS * n * rows * hid_dev,
        ),
    )(
        hidden_states,
        draft_row,
        expert_ids,
        route_weights,
        norm_gain.reshape(1, features),
        w_gate,
        w_up,
        w_down,
    )


def by_size(mesh):
    def run(hidden_states, draft_row, expert_ids, route_weights, norm_gain, w_gate, w_up, w_down):
        ex = mesh.shape["ex"]
        rows = hidden_states.shape[0] // (ex * mesh.shape["grp"])
        every = expert_ids.shape[2] * HID == w_gate.shape[1]
        one_each = w_gate.shape[1] == ex * HID
        features = hidden_states.shape[1]
        shaped = (
            rows * QUARTERS == 16
            and features % 256 == 0
            and (QUARTERS - 1) * PIECE < features // 2 <= QUARTERS * PIECE
        )
        dense = every and one_each and shaped and mesh.shape["tp"] == 2
        in_specs = (
            P(("grp", "ex"), None),
            P(("grp", "ex")),
            P(None, ("grp", "ex"), None),
            P(None, ("grp", "ex"), None),
            P(),
            P(None, ("ex", "tp")),
            P(None, ("ex", "tp")),
            P(("ex", "tp"), None),
        )
        return jax.shard_map(
            fused_shards if dense else shards,
            mesh=mesh,
            in_specs=in_specs,
            out_specs=P(("grp", "ex"), None),
            check_vma=False,
        )(hidden_states, draft_row, expert_ids, route_weights, norm_gain, w_gate, w_up, w_down)

    return run


def solution(mesh):
    return by_size(mesh)
```

```python
import functools

import jax
import jax.numpy as jnp
from jax import lax
from jax.experimental import pallas as pl
from jax.experimental.pallas import tpu as pltpu
from jax.sharding import PartitionSpec as P

HID = 1024
STEPS = 2
RCAP = 2


epsilon = 1e-06


def expert_block(rows_in, w_gate, w_up, w_down):
    gate_proj = jnp.dot(rows_in, w_gate, preferred_element_type=jnp.float32)
    up_proj = jnp.dot(rows_in, w_up, preferred_element_type=jnp.float32)
    activated = (jax.nn.silu(gate_proj) * up_proj).astype(jnp.bfloat16)
    return jnp.dot(activated, w_down, preferred_element_type=jnp.float32)


def fold_back(returned, seating, route_coef, experts, group_size):
    ex_size, slot_cap, columns = returned.shape
    summed = returned.reshape(experts, group_size, slot_cap, columns).sum(axis=1)
    scale = seating.astype(jnp.float32) * route_coef.T[:, None, :]
    return jnp.einsum(
        "ecr,ecd->rd",
        scale,
        summed,
        precision=lax.Precision.HIGHEST,
        preferred_element_type=jnp.float32,
    )


def shards(hidden_states, draft_row, expert_ids, route_weights, norm_gain, w_gate, w_up, w_down):
    row_dev, features = hidden_states.shape
    ex_size = lax.axis_size("ex")
    tp_size = lax.axis_size("tp")
    hid_dev = w_gate.shape[1]
    group_size = HID // (hid_dev * tp_size)
    experts = ex_size // group_size
    chosen_count = expert_ids.shape[2]
    slot_cap = min(row_dev, max(2, 2 * row_dev * chosen_count // experts))
    target_dev = draft_row // row_dev
    target_pos = draft_row % row_dev
    same_dest = target_dev[:, None] == target_dev[None, :]
    earlier = jnp.tril(jnp.ones((row_dev, row_dev), jnp.bool_), -1)
    order_in = jnp.sum(same_dest & earlier, axis=1)
    slot_index = target_dev * RCAP + order_in
    picker = jnp.arange(ex_size * RCAP, dtype=jnp.int32)[:, None] == slot_index[None, :]
    outgoing = (
        jnp.dot(picker.astype(jnp.bfloat16), hidden_states, preferred_element_type=jnp.float32)
        .astype(jnp.bfloat16)
        .reshape(ex_size, RCAP, features)
    )
    labels = (
        jnp.sum(jnp.where(picker, target_pos[None, :] + 1, 0), axis=1)
        .astype(jnp.bfloat16)
        .reshape(ex_size, RCAP)
    )
    arrived, arrived_labels = (
        lax.all_to_all(outgoing, "ex", split_axis=0, concat_axis=0, tiled=True),
        lax.all_to_all(labels, "ex", split_axis=0, concat_axis=0, tiled=True),
    )
    arrived = arrived.reshape(ex_size * RCAP, features)
    settle = (
        arrived_labels.reshape(-1).astype(jnp.float32)[None, :]
        == (jnp.arange(row_dev) + 1).astype(jnp.float32)[:, None]
    )
    current = jnp.dot(
        settle.astype(jnp.bfloat16), arrived, preferred_element_type=jnp.float32
    ).astype(jnp.bfloat16)
    slot_total = ex_size * slot_cap
    for step_no in range(STEPS):
        as_float = current.astype(jnp.float32)
        mean_square = jnp.mean(as_float * as_float, axis=-1, keepdims=True)
        normed = (as_float * lax.rsqrt(mean_square + epsilon) * norm_gain).astype(jnp.bfloat16)
        step_ids = expert_ids[step_no]
        weights = route_weights[step_no]
        matches = step_ids[:, :, None] == jnp.arange(experts, dtype=jnp.int32)[None, None, :]
        chosen = jnp.any(matches, axis=1)
        route_coef = jnp.sum(jnp.where(matches, weights[:, :, None], 0.0), axis=1)
        chosen_int = chosen.astype(jnp.int32)
        before = jnp.cumsum(chosen_int, axis=0) - chosen_int
        seating = chosen.T[:, None, :] & (
            before.T[:, None, :] == jnp.arange(slot_cap, dtype=jnp.int32)[None, :, None]
        )
        packed_base = jnp.einsum(
            "ecr,rd->ecd", seating.astype(jnp.bfloat16), normed, preferred_element_type=jnp.float32
        ).astype(jnp.bfloat16)
        occupancy = jnp.any(seating, axis=2).astype(jnp.bfloat16)
        occupancy = jnp.broadcast_to(occupancy[:, None], (experts, group_size, slot_cap)).reshape(
            ex_size, slot_cap
        )
        packed = jnp.broadcast_to(
            packed_base[:, None], (experts, group_size, slot_cap, features)
        ).reshape(ex_size, slot_cap, features)
        landed, landed_flags = (
            lax.all_to_all(packed, "ex", split_axis=0, concat_axis=0, tiled=True),
            lax.all_to_all(occupancy, "ex", split_axis=0, concat_axis=0, tiled=True),
        )
        rows_in = landed.reshape(slot_total, features)
        partial_value = expert_block(rows_in, w_gate, w_up, w_down)
        returned = lax.all_to_all(
            partial_value.reshape(ex_size, slot_cap, features).astype(jnp.bfloat16),
            "ex",
            split_axis=0,
            concat_axis=0,
            tiled=True,
        ).astype(jnp.float32)
        branch_sum = lax.psum(
            fold_back(returned, seating, route_coef, experts, group_size).astype(jnp.bfloat16), "tp"
        ).astype(jnp.float32)
        current = (current.astype(jnp.float32) + branch_sum).astype(jnp.bfloat16)
    return current


QUARTERS = 4
PIECE = 512
MESH = pl.DeviceIdType.MESH


def one_hot(condition, dtype=jnp.bfloat16):
    return jnp.where(condition, 1.0, 0.0).astype(dtype)


def fused_kernel(
    n,
    hidden_hbm,
    place_hbm,
    ids_hbm,
    weights_hbm,
    gain_hbm,
    wg_hbm,
    wu_hbm,
    wd_hbm,
    out_ref,
    hidden_ref,
    place_ref,
    ids_ref,
    weights_ref,
    gain_ref,
    wg,
    wu,
    wd,
    first,
    second,
    normed,
    swap_out,
    swap_in,
    stage,
    parts_out,
    parts_in,
    coef,
    last,
    small_sem,
    weight_sem,
    gather_send,
    gather_recv,
    pass_send,
    pass_recv,
    swap_send,
    swap_recv,
    back_send,
    back_recv,
    last_send,
    last_recv,
):
    rows, features = hidden_ref.shape
    half = features // 2
    block = QUARTERS * rows
    total = n * rows
    widths = [min(PIECE, half - q * PIECE) for q in range(QUARTERS)]
    grp, me, core = lax.axis_index("grp"), lax.axis_index("ex"), lax.axis_index("tp")
    other = 1 - core

    small = [
        pltpu.make_async_copy(source, target, small_sem.at[i])
        for i, (source, target) in enumerate(
            (
                (hidden_hbm, hidden_ref),
                (place_hbm, place_ref),
                (ids_hbm, ids_ref),
                (weights_hbm, weights_ref),
                (gain_hbm, gain_ref),
            )
        )
    ]
    for copy in small:
        copy.start()
    weight_copies = []
    for h in range(2):
        span = pl.ds(h * half, half)
        for which, (source, target) in enumerate(
            (
                (wg_hbm.at[span, :], wg.at[span, :]),
                (wu_hbm.at[span, :], wu.at[span, :]),
                (wd_hbm.at[:, span], wd.at[h]),
            )
        ):
            weight_copies.append(
                (which, pltpu.make_async_copy(source, target, weight_sem.at[h * 3 + which]))
            )
    for which, copy in sorted(weight_copies, key=lambda pair: pair[0]):
        copy.start()

    barrier = pltpu.get_barrier_semaphore()
    for off in range(1, n):
        pl.semaphore_signal(
            barrier, inc=1, device_id=(grp, lax.rem(me + off, n), core), device_id_type=MESH
        )
    pl.semaphore_signal(barrier, inc=1, device_id=(grp, me, other), device_id_type=MESH)

    mine = pl.ds(pl.multiple_of(me * block, block), block)
    stage[...] = jnp.zeros_like(stage)
    for copy in small:
        copy.wait()
    held = hidden_ref[...].astype(jnp.float32)
    for h in range(2):
        for q in range(QUARTERS):
            start = h * half + q * PIECE
            stage[pl.ds(h * block + q * rows, rows), pl.ds(0, widths[q])] = held[
                :, start : start + widths[q]
            ]
    line = lax.broadcasted_iota(jnp.int32, (block, QUARTERS * total), 0)
    lane = lax.broadcasted_iota(jnp.int32, (block, QUARTERS * total), 1)
    place = jnp.zeros_like(line)
    for r in range(rows):
        place = jnp.where(line % rows == r, place_ref[r], place)
    placing = one_hot((line // rows == lane // total) & (lane % total == place))
    for h in range(2):
        first[h, mine, pl.ds(0, PIECE)] = stage[pl.ds(h * block, block), :].astype(jnp.bfloat16)
        first[h, mine, pl.ds(PIECE, QUARTERS * total)] = placing

    pl.semaphore_wait(barrier, n)

    def gather_start(step, buf):
        sends = []
        for off in range(1, n):
            copy = pltpu.make_async_remote_copy(
                src_ref=buf.at[core, mine, :],
                dst_ref=buf.at[core, mine, :],
                send_sem=gather_send.at[step, off],
                recv_sem=gather_recv.at[step, off],
                device_id=(grp, lax.rem(me + off, n), core),
                device_id_type=MESH,
            )
            copy.start()
            sends.append(copy)
        return sends

    def pass_on(step, buf, off):
        slot = pl.ds(pl.multiple_of(lax.rem(me + n - off, n) * block, block), block)
        copy = pltpu.make_async_remote_copy(
            src_ref=buf.at[core, slot, :],
            dst_ref=buf.at[core, slot, :],
            send_sem=pass_send.at[step, off],
            recv_sem=pass_recv.at[step, off],
            device_id=(grp, me, other),
            device_id_type=MESH,
        )
        copy.start()
        return copy

    pending = []
    sends = gather_start(0, first)
    pending += sends

    for step in range(STEPS):
        ids = ids_ref[step]
        weights = weights_ref[step]
        for e in range(n):
            value = jnp.sum(jnp.where(ids == e, weights, 0.0), axis=1, keepdims=True)
            value = jnp.broadcast_to(value, (rows, 128))
            for q in range(QUARTERS):
                coef[step, e, pl.ds(q * rows, rows), :] = value
    stage[...] = jnp.zeros_like(stage)

    current = None
    for step in range(STEPS):
        buf = first if step == 0 else second
        passes = []
        if step > 0:
            passes.append(pass_on(step, buf, 0))
        for off in range(1, n):
            sends[off - 1].wait_recv()
            passes.append(pass_on(step, buf, off))
        for copy in passes:
            copy.wait_recv()
        pending += passes

        if step == 0:
            pick = jnp.transpose(first[0, :, pl.ds(PIECE, QUARTERS * total)].astype(jnp.float32))
            pick = pick.astype(jnp.bfloat16)
        else:
            to = lax.broadcasted_iota(jnp.int32, (QUARTERS * total, n * block), 0)
            at = lax.broadcasted_iota(jnp.int32, (QUARTERS * total, n * block), 1)
            pick = one_hot(
                (to // total == (at // rows) % QUARTERS)
                & (to % total == (at // block) * rows + at % rows)
            )
        spread = [
            jnp.dot(pick, buf[h, :, pl.ds(0, PIECE)], preferred_element_type=jnp.float32)
            for h in range(2)
        ]
        squares = jnp.sum(spread[0] * spread[0] + spread[1] * spread[1], axis=1, keepdims=True)
        square = squares[0:total]
        for q in range(1, QUARTERS):
            square = square + squares[q * total : (q + 1) * total]
        scale = lax.rsqrt(square / features + epsilon)
        for h in range(2):
            for q in range(QUARTERS):
                start = h * half + q * PIECE
                piece = spread[h][q * total : (q + 1) * total, : widths[q]]
                gain = gain_ref[pl.ds(start, widths[q])].reshape(1, widths[q])
                normed[:, pl.ds(start, widths[q])] = (piece * scale * gain).astype(jnp.bfloat16)
        if step == 0:
            for which, copy in weight_copies:
                if which < 2:
                    copy.wait()
        gate = jnp.dot(normed[...], wg[...], preferred_element_type=jnp.float32)
        up = jnp.dot(normed[...], wu[...], preferred_element_type=jnp.float32)
        act = (gate / (1.0 + jnp.exp(-gate)) * up).astype(jnp.bfloat16)
        if step == 0:
            for which, copy in weight_copies:
                if which == 2:
                    copy.wait()
        for q in range(QUARTERS):
            cols = pl.ds(q * PIECE, widths[q])
            swap_out[step, :, cols] = jnp.dot(
                act, wd[other, :, cols], preferred_element_type=jnp.float32
            ).astype(jnp.bfloat16)
        swap = pltpu.make_async_remote_copy(
            src_ref=swap_out.at[step],
            dst_ref=swap_in.at[step],
            send_sem=swap_send.at[step],
            recv_sem=swap_recv.at[step],
            device_id=(grp, me, other),
            device_id_type=MESH,
        )
        swap.start()
        own = [
            jnp.dot(
                act, wd[core, :, pl.ds(q * PIECE, widths[q])], preferred_element_type=jnp.float32
            )
            for q in range(QUARTERS)
        ]
        if step == 0:
            to = lax.broadcasted_iota(jnp.int32, (block, QUARTERS * total), 0)
            at = lax.broadcasted_iota(jnp.int32, (block, QUARTERS * total), 1)
            keep = one_hot((to // rows == at // total) & (at % total == me * rows + to % rows))
            spread_own = jnp.where(core == 0, spread[0], spread[1]).astype(jnp.bfloat16)
            current = jnp.dot(keep, spread_own, preferred_element_type=jnp.float32)
        swap.wait_recv()
        pending.append(swap)
        for q in range(QUARTERS):
            cols = pl.ds(q * PIECE, widths[q])
            value = own[q] + swap_in[step, :, cols].astype(jnp.float32)
            for p in range(n):
                stage[pl.ds(p * block + q * rows, rows), pl.ds(0, widths[q])] = value[
                    p * rows : (p + 1) * rows
                ]
        parts_out[step] = stage[...].astype(jnp.bfloat16)
        backs = []
        for off in range(1, n):
            peer = lax.rem(me + off, n)
            copy = pltpu.make_async_remote_copy(
                src_ref=parts_out.at[step, pl.ds(pl.multiple_of(peer * block, block), block), :],
                dst_ref=parts_in.at[step, mine, :],
                send_sem=back_send.at[step, off],
                recv_sem=back_recv.at[step, off],
                device_id=(grp, peer, core),
                device_id_type=MESH,
            )
            copy.start()
            backs.append(copy)
        parts_in[step, mine, :] = parts_out[step, mine, :]
        for copy in backs:
            copy.wait_recv()
        pending += backs
        moe = None
        for e in range(n):
            value = parts_in[step, pl.ds(e * block, block), :].astype(jnp.float32)
            value = value * jnp.concatenate([coef[step, e]] * (PIECE // 128), axis=1)
            moe = value if moe is None else moe + value
        result = (current + moe).astype(jnp.bfloat16)
        current = result.astype(jnp.float32)
        if step < STEPS - 1:
            second[core, mine, :] = result
            sends = gather_start(step + 1, second)
            pending += sends

    last[core] = result
    final = pltpu.make_async_remote_copy(
        src_ref=last.at[core],
        dst_ref=last.at[core],
        send_sem=last_send,
        recv_sem=last_recv,
        device_id=(grp, me, other),
        device_id_type=MESH,
    )
    final.start()
    final.wait_recv()
    pending.append(final)
    for h in range(2):
        value = last[h].astype(jnp.float32)
        for q in range(QUARTERS):
            out_ref[:, pl.ds(h * half + q * PIECE, widths[q])] = value[
                q * rows : (q + 1) * rows, : widths[q]
            ].astype(jnp.bfloat16)
    for copy in pending:
        copy.wait_send()


def fused_shards(hidden_states, draft_row, expert_ids, route_weights, norm_gain, w_gate, w_up, w_down):
    rows, features = hidden_states.shape
    hid_dev = w_gate.shape[1]
    n = lax.axis_size("ex")
    block = QUARTERS * rows
    half = features // 2
    spread = QUARTERS * n * rows
    vmem, hbm = pl.BlockSpec(memory_space=pltpu.VMEM), pl.BlockSpec(memory_space=pltpu.HBM)
    dma = pltpu.SemaphoreType.DMA
    return pl.pallas_call(
        functools.partial(fused_kernel, n),
        out_shape=jax.ShapeDtypeStruct((rows, features), jnp.bfloat16),
        in_specs=[hbm] * 8,
        out_specs=vmem,
        scratch_shapes=[
            pltpu.VMEM((rows, features), jnp.bfloat16),
            pltpu.SMEM((rows,), jnp.int32),
            pltpu.VMEM(expert_ids.shape, jnp.int32),
            pltpu.VMEM(route_weights.shape, jnp.float32),
            pltpu.VMEM((features,), jnp.float32),
            pltpu.VMEM((features, hid_dev), jnp.bfloat16),
            pltpu.VMEM((features, hid_dev), jnp.bfloat16),
            pltpu.VMEM((2, hid_dev, half), jnp.bfloat16),
            pltpu.VMEM((2, n * block, PIECE + spread), jnp.bfloat16),
            pltpu.VMEM((2, n * block, PIECE), jnp.bfloat16),
            pltpu.VMEM((n * rows, features), jnp.bfloat16),
            pltpu.VMEM((STEPS, n * rows, half), jnp.bfloat16),
            pltpu.VMEM((STEPS, n * rows, half), jnp.bfloat16),
            pltpu.VMEM((n * block, PIECE), jnp.float32),
            pltpu.VMEM((STEPS, n * block, PIECE), jnp.bfloat16),
            pltpu.VMEM((STEPS, n * block, PIECE), jnp.bfloat16),
            pltpu.VMEM((STEPS, n, block, 128), jnp.float32),
            pltpu.VMEM((2, block, PIECE), jnp.bfloat16),
            dma((5,)),
            dma((6,)),
            dma((STEPS, n)),
            dma((STEPS, n)),
            dma((STEPS, n)),
            dma((STEPS, n)),
            dma((STEPS,)),
            dma((STEPS,)),
            dma((STEPS, n)),
            dma((STEPS, n)),
            dma,
            dma,
        ],
        compiler_params=pltpu.CompilerParams(
            collective_id=0, has_side_effects=True, vmem_limit_bytes=63 * 1024 * 1024
        ),
        cost_estimate=pl.CostEstimate(
            flops=STEPS * 6 * n * rows * features * hid_dev,
            bytes_accessed=6 * features * hid_dev,
            transcendentals=STEPS * n * rows * hid_dev,
        ),
    )(
        hidden_states,
        draft_row,
        expert_ids,
        route_weights,
        norm_gain,
        w_gate,
        w_up,
        w_down,
    )


def by_size(mesh):
    def run(hidden_states, draft_row, expert_ids, route_weights, norm_gain, w_gate, w_up, w_down):
        ex = mesh.shape["ex"]
        rows = hidden_states.shape[0] // (ex * mesh.shape["grp"])
        every = expert_ids.shape[2] * HID == w_gate.shape[1]
        one_each = w_gate.shape[1] == ex * HID
        features = hidden_states.shape[1]
        shaped = (
            rows * QUARTERS == 16
            and features % 256 == 0
            and (QUARTERS - 1) * PIECE < features // 2 <= QUARTERS * PIECE
        )
        dense = every and one_each and shaped and mesh.shape["tp"] == 2
        in_specs = (
            P(("grp", "ex"), None),
            P(("grp", "ex")),
            P(None, ("grp", "ex"), None),
            P(None, ("grp", "ex"), None),
            P(),
            P(None, ("ex", "tp")),
            P(None, ("ex", "tp")),
            P(("ex", "tp"), None),
        )
        return jax.shard_map(
            fused_shards if dense else shards,
            mesh=mesh,
            in_specs=in_specs,
            out_specs=P(("grp", "ex"), None),
            check_vma=False,
        )(hidden_states, draft_row, expert_ids, route_weights, norm_gain, w_gate, w_up, w_down)

    return run


def solution(mesh):
    return by_size(mesh)
```

```python
import functools

import jax
import jax.numpy as jnp
from jax import lax
from jax.experimental import pallas as pl
from jax.experimental.pallas import tpu as pltpu
from jax.sharding import PartitionSpec as P

HID = 1024
STEPS = 2
RCAP = 2


epsilon = 1e-06


def expert_block(rows_in, w_gate, w_up, w_down):
    gate_proj = jnp.dot(rows_in, w_gate, preferred_element_type=jnp.float32)
    up_proj = jnp.dot(rows_in, w_up, preferred_element_type=jnp.float32)
    activated = (jax.nn.silu(gate_proj) * up_proj).astype(jnp.bfloat16)
    return jnp.dot(activated, w_down, preferred_element_type=jnp.float32)


def fold_back(returned, seating, route_coef, experts, group_size):
    ex_size, slot_cap, columns = returned.shape
    summed = returned.reshape(experts, group_size, slot_cap, columns).sum(axis=1)
    scale = seating.astype(jnp.float32) * route_coef.T[:, None, :]
    return jnp.einsum(
        "ecr,ecd->rd",
        scale,
        summed,
        precision=lax.Precision.HIGHEST,
        preferred_element_type=jnp.float32,
    )


def shards(hidden_states, draft_row, expert_ids, route_weights, norm_gain, w_gate, w_up, w_down):
    row_dev, features = hidden_states.shape
    ex_size = lax.axis_size("ex")
    tp_size = lax.axis_size("tp")
    hid_dev = w_gate.shape[1]
    group_size = HID // (hid_dev * tp_size)
    experts = ex_size // group_size
    chosen_count = expert_ids.shape[2]
    slot_cap = min(row_dev, max(2, 2 * row_dev * chosen_count // experts))
    target_dev = draft_row // row_dev
    target_pos = draft_row % row_dev
    same_dest = target_dev[:, None] == target_dev[None, :]
    earlier = jnp.tril(jnp.ones((row_dev, row_dev), jnp.bool_), -1)
    order_in = jnp.sum(same_dest & earlier, axis=1)
    slot_index = target_dev * RCAP + order_in
    picker = jnp.arange(ex_size * RCAP, dtype=jnp.int32)[:, None] == slot_index[None, :]
    outgoing = (
        jnp.dot(picker.astype(jnp.bfloat16), hidden_states, preferred_element_type=jnp.float32)
        .astype(jnp.bfloat16)
        .reshape(ex_size, RCAP, features)
    )
    labels = (
        jnp.sum(jnp.where(picker, target_pos[None, :] + 1, 0), axis=1)
        .astype(jnp.bfloat16)
        .reshape(ex_size, RCAP)
    )
    arrived, arrived_labels = (
        lax.all_to_all(outgoing, "ex", split_axis=0, concat_axis=0, tiled=True),
        lax.all_to_all(labels, "ex", split_axis=0, concat_axis=0, tiled=True),
    )
    arrived = arrived.reshape(ex_size * RCAP, features)
    settle = (
        arrived_labels.reshape(-1).astype(jnp.float32)[None, :]
        == (jnp.arange(row_dev) + 1).astype(jnp.float32)[:, None]
    )
    current = jnp.dot(
        settle.astype(jnp.bfloat16), arrived, preferred_element_type=jnp.float32
    ).astype(jnp.bfloat16)
    slot_total = ex_size * slot_cap
    for step_no in range(STEPS):
        as_float = current.astype(jnp.float32)
        mean_square = jnp.mean(as_float * as_float, axis=-1, keepdims=True)
        normed = (as_float * lax.rsqrt(mean_square + epsilon) * norm_gain).astype(jnp.bfloat16)
        step_ids = expert_ids[step_no]
        weights = route_weights[step_no]
        matches = step_ids[:, :, None] == jnp.arange(experts, dtype=jnp.int32)[None, None, :]
        chosen = jnp.any(matches, axis=1)
        route_coef = jnp.sum(jnp.where(matches, weights[:, :, None], 0.0), axis=1)
        chosen_int = chosen.astype(jnp.int32)
        before = jnp.cumsum(chosen_int, axis=0) - chosen_int
        seating = chosen.T[:, None, :] & (
            before.T[:, None, :] == jnp.arange(slot_cap, dtype=jnp.int32)[None, :, None]
        )
        packed_base = jnp.einsum(
            "ecr,rd->ecd", seating.astype(jnp.bfloat16), normed, preferred_element_type=jnp.float32
        ).astype(jnp.bfloat16)
        occupancy = jnp.any(seating, axis=2).astype(jnp.bfloat16)
        occupancy = jnp.broadcast_to(occupancy[:, None], (experts, group_size, slot_cap)).reshape(
            ex_size, slot_cap
        )
        packed = jnp.broadcast_to(
            packed_base[:, None], (experts, group_size, slot_cap, features)
        ).reshape(ex_size, slot_cap, features)
        landed, landed_flags = (
            lax.all_to_all(packed, "ex", split_axis=0, concat_axis=0, tiled=True),
            lax.all_to_all(occupancy, "ex", split_axis=0, concat_axis=0, tiled=True),
        )
        rows_in = landed.reshape(slot_total, features)
        partial_value = expert_block(rows_in, w_gate, w_up, w_down)
        returned = lax.all_to_all(
            partial_value.reshape(ex_size, slot_cap, features).astype(jnp.bfloat16),
            "ex",
            split_axis=0,
            concat_axis=0,
            tiled=True,
        ).astype(jnp.float32)
        branch_sum = lax.psum(
            fold_back(returned, seating, route_coef, experts, group_size).astype(jnp.bfloat16), "tp"
        ).astype(jnp.float32)
        current = (current.astype(jnp.float32) + branch_sum).astype(jnp.bfloat16)
    return current


QUARTERS = 4
PIECE = 512
MESH = pl.DeviceIdType.MESH


def one_hot(condition, dtype=jnp.bfloat16):
    return jnp.where(condition, 1.0, 0.0).astype(dtype)


def fused_kernel(
    n,
    hidden_hbm,
    place_hbm,
    ids_hbm,
    weights_hbm,
    gain_hbm,
    wg_hbm,
    wu_hbm,
    wd_hbm,
    out_ref,
    hidden_ref,
    place_ref,
    ids_ref,
    weights_ref,
    gain_ref,
    wg,
    wu,
    wd,
    first,
    second,
    ordered,
    normed,
    swap_out,
    swap_in,
    stage,
    parts_out,
    parts_in,
    coef,
    last,
    small_sem,
    weight_sem,
    gather_send,
    gather_recv,
    pass_send,
    pass_recv,
    swap_send,
    swap_recv,
    back_send,
    back_recv,
    last_send,
    last_recv,
):
    rows, features = hidden_ref.shape
    half = features // 2
    block = QUARTERS * rows
    total = n * rows
    widths = [min(PIECE, half - q * PIECE) for q in range(QUARTERS)]
    grp, me, core = lax.axis_index("grp"), lax.axis_index("ex"), lax.axis_index("tp")
    other = 1 - core

    small = [
        pltpu.make_async_copy(source, target, small_sem.at[i])
        for i, (source, target) in enumerate(
            (
                (hidden_hbm, hidden_ref),
                (place_hbm, place_ref),
                (ids_hbm, ids_ref),
                (weights_hbm, weights_ref),
                (gain_hbm, gain_ref),
            )
        )
    ]
    for copy in small:
        copy.start()
    weight_copies = []
    for h in range(2):
        span = pl.ds(h * half, half)
        for which, (source, target) in enumerate(
            (
                (wg_hbm.at[span, :], wg.at[h]),
                (wu_hbm.at[span, :], wu.at[h]),
                (wd_hbm.at[:, span], wd.at[h]),
            )
        ):
            weight_copies.append(
                pltpu.make_async_copy(source, target, weight_sem.at[h * 3 + which])
            )
    for i in (0, 3, 1, 4, 2, 5):
        weight_copies[i].start()

    barrier = pltpu.get_barrier_semaphore()
    for off in range(1, n):
        pl.semaphore_signal(
            barrier, inc=1, device_id=(grp, lax.rem(me + off, n), core), device_id_type=MESH
        )
    pl.semaphore_signal(barrier, inc=1, device_id=(grp, me, other), device_id_type=MESH)

    mine = pl.ds(pl.multiple_of(me * block, block), block)
    stage[...] = jnp.zeros_like(stage)
    for copy in small:
        copy.wait()
    held = hidden_ref[...].astype(jnp.float32)
    for h in range(2):
        for q in range(QUARTERS):
            start = h * half + q * PIECE
            stage[pl.ds(h * block + q * rows, rows), pl.ds(0, widths[q])] = held[
                :, start : start + widths[q]
            ]
    line = lax.broadcasted_iota(jnp.int32, (block, QUARTERS * total), 0)
    lane = lax.broadcasted_iota(jnp.int32, (block, QUARTERS * total), 1)
    place = jnp.zeros_like(line)
    for r in range(rows):
        place = jnp.where(line % rows == r, place_ref[r], place)
    placing = one_hot((line // rows == lane // total) & (lane % total == place))
    for h in range(2):
        first[h, mine, pl.ds(0, PIECE)] = stage[pl.ds(h * block, block), :].astype(jnp.bfloat16)
        first[h, mine, pl.ds(PIECE, QUARTERS * total)] = placing

    pl.semaphore_wait(barrier, n)

    def gather_start(step, buf):
        sends = []
        for off in range(1, n):
            copy = pltpu.make_async_remote_copy(
                src_ref=buf.at[core, mine, :],
                dst_ref=buf.at[core, mine, :],
                send_sem=gather_send.at[step, off],
                recv_sem=gather_recv.at[step, off],
                device_id=(grp, lax.rem(me + off, n), core),
                device_id_type=MESH,
            )
            copy.start()
            sends.append(copy)
        return sends

    def pass_on(step, buf, off):
        slot = pl.ds(pl.multiple_of(lax.rem(me + n - off, n) * block, block), block)
        copy = pltpu.make_async_remote_copy(
            src_ref=buf.at[core, slot, :],
            dst_ref=buf.at[core, slot, :],
            send_sem=pass_send.at[step, off],
            recv_sem=pass_recv.at[step, off],
            device_id=(grp, me, other),
            device_id_type=MESH,
        )
        copy.start()
        return copy

    pending = []
    sends = gather_start(0, first)
    pending += sends

    for step in range(STEPS):
        ids = ids_ref[step]
        weights = weights_ref[step]
        for e in range(n):
            value = jnp.sum(jnp.where(ids == e, weights, 0.0), axis=1, keepdims=True)
            value = jnp.broadcast_to(value, (rows, 128))
            for q in range(QUARTERS):
                coef[step, e, pl.ds(q * rows, rows), :] = value
    stage[...] = jnp.zeros_like(stage)
    to = lax.broadcasted_iota(jnp.int32, (QUARTERS * total, n * block), 0)
    at = lax.broadcasted_iota(jnp.int32, (QUARTERS * total, n * block), 1)
    ordered[...] = one_hot(
        (to // total == (at // rows) % QUARTERS)
        & (to % total == (at // block) * rows + at % rows)
    )
    for copy in weight_copies[0:2] + weight_copies[3:5]:
        copy.wait()

    def half_product(buf, h, pick):
        spread = jnp.dot(pick, buf[h, :, pl.ds(0, PIECE)], preferred_element_type=jnp.float32)
        squares = jnp.sum(spread * spread, axis=1, keepdims=True)
        square = squares[0:total]
        for q in range(1, QUARTERS):
            square = square + squares[q * total : (q + 1) * total]
        scale = lax.rsqrt(square / half + epsilon)
        for q in range(QUARTERS):
            gains = [
                gain_ref[pl.ds(side * half + q * PIECE, widths[q])].reshape(1, widths[q])
                for side in range(2)
            ]
            gain = jnp.where(h == 0, gains[0], gains[1])
            piece = spread[q * total : (q + 1) * total, : widths[q]]
            normed[h, :, pl.ds(q * PIECE, widths[q])] = (piece * scale * gain).astype(jnp.bfloat16)
        gate = jnp.dot(normed[h], wg[h], preferred_element_type=jnp.float32)
        up = jnp.dot(normed[h], wu[h], preferred_element_type=jnp.float32)
        return spread, square, scale, gate, up

    current = None
    for step in range(STEPS):
        buf = first if step == 0 else second
        passes = []
        if step > 0:
            passes.append(pass_on(step, buf, 0))
        for off in range(1, n):
            sends[off - 1].wait_recv()
            passes.append(pass_on(step, buf, off))
        pending += passes
        if step == 0:
            pick = jnp.transpose(
                first[core, :, pl.ds(PIECE, QUARTERS * total)].astype(jnp.float32)
            ).astype(jnp.bfloat16)
        else:
            pick = ordered[...]
        spread_own, square_own, scale_own, gate_own, up_own = half_product(buf, core, pick)
        for copy in passes:
            copy.wait_recv()
        _, square_other, scale_other, gate_other, up_other = half_product(buf, other, pick)
        scale = lax.rsqrt((square_own + square_other) / features + epsilon)
        fit_own = jnp.where(scale == 0.0, 0.0, scale / scale_own)
        fit_other = jnp.where(scale == 0.0, 0.0, scale / scale_other)
        gate = gate_own * fit_own + gate_other * fit_other
        up = up_own * fit_own + up_other * fit_other
        act = (gate / (1.0 + jnp.exp(-gate)) * up).astype(jnp.bfloat16)
        if step == 0:
            for copy in weight_copies[2::3]:
                copy.wait()
        for q in range(QUARTERS):
            cols = pl.ds(q * PIECE, widths[q])
            swap_out[step, :, cols] = jnp.dot(
                act, wd[other, :, cols], preferred_element_type=jnp.float32
            ).astype(jnp.bfloat16)
        swap = pltpu.make_async_remote_copy(
            src_ref=swap_out.at[step],
            dst_ref=swap_in.at[step],
            send_sem=swap_send.at[step],
            recv_sem=swap_recv.at[step],
            device_id=(grp, me, other),
            device_id_type=MESH,
        )
        swap.start()
        own = [
            jnp.dot(
                act, wd[core, :, pl.ds(q * PIECE, widths[q])], preferred_element_type=jnp.float32
            )
            for q in range(QUARTERS)
        ]
        if step == 0:
            to = lax.broadcasted_iota(jnp.int32, (block, QUARTERS * total), 0)
            at = lax.broadcasted_iota(jnp.int32, (block, QUARTERS * total), 1)
            keep = one_hot((to // rows == at // total) & (at % total == me * rows + to % rows))
            current = jnp.dot(
                keep, spread_own.astype(jnp.bfloat16), preferred_element_type=jnp.float32
            )
        swap.wait_recv()
        pending.append(swap)
        for q in range(QUARTERS):
            cols = pl.ds(q * PIECE, widths[q])
            value = own[q] + swap_in[step, :, cols].astype(jnp.float32)
            for p in range(n):
                stage[pl.ds(p * block + q * rows, rows), pl.ds(0, widths[q])] = value[
                    p * rows : (p + 1) * rows
                ]
        parts_out[step] = stage[...].astype(jnp.bfloat16)
        backs = []
        for off in range(1, n):
            peer = lax.rem(me + off, n)
            copy = pltpu.make_async_remote_copy(
                src_ref=parts_out.at[step, pl.ds(pl.multiple_of(peer * block, block), block), :],
                dst_ref=parts_in.at[step, mine, :],
                send_sem=back_send.at[step, off],
                recv_sem=back_recv.at[step, off],
                device_id=(grp, peer, core),
                device_id_type=MESH,
            )
            copy.start()
            backs.append(copy)
        parts_in[step, mine, :] = parts_out[step, mine, :]
        for copy in backs:
            copy.wait_recv()
        pending += backs
        moe = None
        for e in range(n):
            value = parts_in[step, pl.ds(e * block, block), :].astype(jnp.float32)
            value = value * jnp.concatenate([coef[step, e]] * (PIECE // 128), axis=1)
            moe = value if moe is None else moe + value
        result = (current + moe).astype(jnp.bfloat16)
        current = result.astype(jnp.float32)
        if step < STEPS - 1:
            second[core, mine, :] = result
            sends = gather_start(step + 1, second)
            pending += sends

    last[core] = result
    final = pltpu.make_async_remote_copy(
        src_ref=last.at[core],
        dst_ref=last.at[core],
        send_sem=last_send,
        recv_sem=last_recv,
        device_id=(grp, me, other),
        device_id_type=MESH,
    )
    final.start()
    final.wait_recv()
    pending.append(final)
    for h in range(2):
        value = last[h].astype(jnp.float32)
        for q in range(QUARTERS):
            out_ref[:, pl.ds(h * half + q * PIECE, widths[q])] = value[
                q * rows : (q + 1) * rows, : widths[q]
            ].astype(jnp.bfloat16)
    for copy in pending:
        copy.wait_send()


def fused_shards(hidden_states, draft_row, expert_ids, route_weights, norm_gain, w_gate, w_up, w_down):
    rows, features = hidden_states.shape
    hid_dev = w_gate.shape[1]
    n = lax.axis_size("ex")
    block = QUARTERS * rows
    half = features // 2
    spread = QUARTERS * n * rows
    vmem, hbm = pl.BlockSpec(memory_space=pltpu.VMEM), pl.BlockSpec(memory_space=pltpu.HBM)
    dma = pltpu.SemaphoreType.DMA
    return pl.pallas_call(
        functools.partial(fused_kernel, n),
        out_shape=jax.ShapeDtypeStruct((rows, features), jnp.bfloat16),
        in_specs=[hbm] * 8,
        out_specs=vmem,
        scratch_shapes=[
            pltpu.VMEM((rows, features), jnp.bfloat16),
            pltpu.SMEM((rows,), jnp.int32),
            pltpu.VMEM(expert_ids.shape, jnp.int32),
            pltpu.VMEM(route_weights.shape, jnp.float32),
            pltpu.VMEM((features,), jnp.float32),
            pltpu.VMEM((2, half, hid_dev), jnp.bfloat16),
            pltpu.VMEM((2, half, hid_dev), jnp.bfloat16),
            pltpu.VMEM((2, hid_dev, half), jnp.bfloat16),
            pltpu.VMEM((2, n * block, PIECE + spread), jnp.bfloat16),
            pltpu.VMEM((2, n * block, PIECE), jnp.bfloat16),
            pltpu.VMEM((spread, n * block), jnp.bfloat16),
            pltpu.VMEM((2, n * rows, half), jnp.bfloat16),
            pltpu.VMEM((STEPS, n * rows, half), jnp.bfloat16),
            pltpu.VMEM((STEPS, n * rows, half), jnp.bfloat16),
            pltpu.VMEM((n * block, PIECE), jnp.float32),
            pltpu.VMEM((STEPS, n * block, PIECE), jnp.bfloat16),
            pltpu.VMEM((STEPS, n * block, PIECE), jnp.bfloat16),
            pltpu.VMEM((STEPS, n, block, 128), jnp.float32),
            pltpu.VMEM((2, block, PIECE), jnp.bfloat16),
            dma((5,)),
            dma((6,)),
            dma((STEPS, n)),
            dma((STEPS, n)),
            dma((STEPS, n)),
            dma((STEPS, n)),
            dma((STEPS,)),
            dma((STEPS,)),
            dma((STEPS, n)),
            dma((STEPS, n)),
            dma,
            dma,
        ],
        compiler_params=pltpu.CompilerParams(
            collective_id=0, has_side_effects=True, vmem_limit_bytes=63 * 1024 * 1024
        ),
        cost_estimate=pl.CostEstimate(
            flops=STEPS * 6 * n * rows * features * hid_dev,
            bytes_accessed=6 * features * hid_dev,
            transcendentals=STEPS * n * rows * hid_dev,
        ),
    )(
        hidden_states,
        draft_row,
        expert_ids,
        route_weights,
        norm_gain,
        w_gate,
        w_up,
        w_down,
    )


def by_size(mesh):
    def run(hidden_states, draft_row, expert_ids, route_weights, norm_gain, w_gate, w_up, w_down):
        ex = mesh.shape["ex"]
        rows = hidden_states.shape[0] // (ex * mesh.shape["grp"])
        every = expert_ids.shape[2] * HID == w_gate.shape[1]
        one_each = w_gate.shape[1] == ex * HID
        features = hidden_states.shape[1]
        shaped = (
            rows * QUARTERS == 16
            and features % 256 == 0
            and (QUARTERS - 1) * PIECE < features // 2 <= QUARTERS * PIECE
        )
        dense = every and one_each and shaped and mesh.shape["tp"] == 2
        in_specs = (
            P(("grp", "ex"), None),
            P(("grp", "ex")),
            P(None, ("grp", "ex"), None),
            P(None, ("grp", "ex"), None),
            P(),
            P(None, ("ex", "tp")),
            P(None, ("ex", "tp")),
            P(("ex", "tp"), None),
        )
        return jax.shard_map(
            fused_shards if dense else shards,
            mesh=mesh,
            in_specs=in_specs,
            out_specs=P(("grp", "ex"), None),
            check_vma=False,
        )(hidden_states, draft_row, expert_ids, route_weights, norm_gain, w_gate, w_up, w_down)

    return run


def solution(mesh):
    return by_size(mesh)
```

```python
import functools

import jax
import jax.numpy as jnp
from jax import lax
from jax.experimental import pallas as pl
from jax.experimental.pallas import tpu as pltpu
from jax.sharding import PartitionSpec as P

HID = 1024
STEPS = 2
RCAP = 2


epsilon = 1e-06


def expert_block(rows_in, w_gate, w_up, w_down):
    gate_proj = jnp.dot(rows_in, w_gate, preferred_element_type=jnp.float32)
    up_proj = jnp.dot(rows_in, w_up, preferred_element_type=jnp.float32)
    activated = (jax.nn.silu(gate_proj) * up_proj).astype(jnp.bfloat16)
    return jnp.dot(activated, w_down, preferred_element_type=jnp.float32)


def fold_back(returned, seating, route_coef, experts, group_size):
    ex_size, slot_cap, columns = returned.shape
    summed = returned.reshape(experts, group_size, slot_cap, columns).sum(axis=1)
    scale = seating.astype(jnp.float32) * route_coef.T[:, None, :]
    return jnp.einsum(
        "ecr,ecd->rd",
        scale,
        summed,
        precision=lax.Precision.HIGHEST,
        preferred_element_type=jnp.float32,
    )


def shards(hidden_states, draft_row, expert_ids, route_weights, norm_gain, w_gate, w_up, w_down):
    row_dev, features = hidden_states.shape
    ex_size = lax.axis_size("ex")
    tp_size = lax.axis_size("tp")
    hid_dev = w_gate.shape[1]
    group_size = HID // (hid_dev * tp_size)
    experts = ex_size // group_size
    chosen_count = expert_ids.shape[2]
    slot_cap = min(row_dev, max(2, 2 * row_dev * chosen_count // experts))
    target_dev = draft_row // row_dev
    target_pos = draft_row % row_dev
    same_dest = target_dev[:, None] == target_dev[None, :]
    earlier = jnp.tril(jnp.ones((row_dev, row_dev), jnp.bool_), -1)
    order_in = jnp.sum(same_dest & earlier, axis=1)
    slot_index = target_dev * RCAP + order_in
    picker = jnp.arange(ex_size * RCAP, dtype=jnp.int32)[:, None] == slot_index[None, :]
    outgoing = (
        jnp.dot(picker.astype(jnp.bfloat16), hidden_states, preferred_element_type=jnp.float32)
        .astype(jnp.bfloat16)
        .reshape(ex_size, RCAP, features)
    )
    labels = (
        jnp.sum(jnp.where(picker, target_pos[None, :] + 1, 0), axis=1)
        .astype(jnp.bfloat16)
        .reshape(ex_size, RCAP)
    )
    arrived, arrived_labels = (
        lax.all_to_all(outgoing, "ex", split_axis=0, concat_axis=0, tiled=True),
        lax.all_to_all(labels, "ex", split_axis=0, concat_axis=0, tiled=True),
    )
    arrived = arrived.reshape(ex_size * RCAP, features)
    settle = (
        arrived_labels.reshape(-1).astype(jnp.float32)[None, :]
        == (jnp.arange(row_dev) + 1).astype(jnp.float32)[:, None]
    )
    current = jnp.dot(
        settle.astype(jnp.bfloat16), arrived, preferred_element_type=jnp.float32
    ).astype(jnp.bfloat16)
    slot_total = ex_size * slot_cap
    for step_no in range(STEPS):
        as_float = current.astype(jnp.float32)
        mean_square = jnp.mean(as_float * as_float, axis=-1, keepdims=True)
        normed = (as_float * lax.rsqrt(mean_square + epsilon) * norm_gain).astype(jnp.bfloat16)
        step_ids = expert_ids[step_no]
        weights = route_weights[step_no]
        matches = step_ids[:, :, None] == jnp.arange(experts, dtype=jnp.int32)[None, None, :]
        chosen = jnp.any(matches, axis=1)
        route_coef = jnp.sum(jnp.where(matches, weights[:, :, None], 0.0), axis=1)
        chosen_int = chosen.astype(jnp.int32)
        before = jnp.cumsum(chosen_int, axis=0) - chosen_int
        seating = chosen.T[:, None, :] & (
            before.T[:, None, :] == jnp.arange(slot_cap, dtype=jnp.int32)[None, :, None]
        )
        packed_base = jnp.einsum(
            "ecr,rd->ecd", seating.astype(jnp.bfloat16), normed, preferred_element_type=jnp.float32
        ).astype(jnp.bfloat16)
        occupancy = jnp.any(seating, axis=2).astype(jnp.bfloat16)
        occupancy = jnp.broadcast_to(occupancy[:, None], (experts, group_size, slot_cap)).reshape(
            ex_size, slot_cap
        )
        packed = jnp.broadcast_to(
            packed_base[:, None], (experts, group_size, slot_cap, features)
        ).reshape(ex_size, slot_cap, features)
        landed, landed_flags = (
            lax.all_to_all(packed, "ex", split_axis=0, concat_axis=0, tiled=True),
            lax.all_to_all(occupancy, "ex", split_axis=0, concat_axis=0, tiled=True),
        )
        rows_in = landed.reshape(slot_total, features)
        partial_value = expert_block(rows_in, w_gate, w_up, w_down)
        returned = lax.all_to_all(
            partial_value.reshape(ex_size, slot_cap, features).astype(jnp.bfloat16),
            "ex",
            split_axis=0,
            concat_axis=0,
            tiled=True,
        ).astype(jnp.float32)
        branch_sum = lax.psum(
            fold_back(returned, seating, route_coef, experts, group_size).astype(jnp.bfloat16), "tp"
        ).astype(jnp.float32)
        current = (current.astype(jnp.float32) + branch_sum).astype(jnp.bfloat16)
    return current


QUARTERS = 4
PIECE = 512
CHUNKS = 2
MESH = pl.DeviceIdType.MESH


def one_hot(condition, dtype=jnp.bfloat16):
    return jnp.where(condition, 1.0, 0.0).astype(dtype)


def fused_kernel(
    n,
    hidden_hbm,
    place_hbm,
    ids_hbm,
    weights_hbm,
    gain_hbm,
    wg_hbm,
    wu_hbm,
    wd_hbm,
    out_ref,
    hidden_ref,
    place_ref,
    ids_ref,
    weights_ref,
    gain_ref,
    wg,
    wu,
    wd,
    first,
    second,
    ordered,
    normed,
    swap_out,
    swap_in,
    stage,
    parts_out,
    parts_in,
    coef,
    last,
    small_sem,
    weight_sem,
    gather_send,
    gather_recv,
    pass_send,
    pass_recv,
    swap_send,
    swap_recv,
    back_send,
    back_recv,
    last_send,
    last_recv,
):
    rows, features = hidden_ref.shape
    half = features // 2
    block = QUARTERS * rows
    total = n * rows
    widths = [min(PIECE, half - q * PIECE) for q in range(QUARTERS)]
    grp, me, core = lax.axis_index("grp"), lax.axis_index("ex"), lax.axis_index("tp")
    other = 1 - core

    small = [
        pltpu.make_async_copy(source, target, small_sem.at[i])
        for i, (source, target) in enumerate(
            (
                (hidden_hbm, hidden_ref),
                (place_hbm, place_ref),
                (ids_hbm, ids_ref),
                (weights_hbm, weights_ref),
                (gain_hbm, gain_ref),
            )
        )
    ]
    for copy in small:
        copy.start()
    weight_copies = []
    for h in range(2):
        span = pl.ds(h * half, half)
        for which, (source, target) in enumerate(
            (
                (wg_hbm.at[span, :], wg.at[h]),
                (wu_hbm.at[span, :], wu.at[h]),
                (wd_hbm.at[:, span], wd.at[h]),
            )
        ):
            weight_copies.append(
                pltpu.make_async_copy(source, target, weight_sem.at[h * 3 + which])
            )
    for i in (0, 3, 1, 4, 2, 5):
        weight_copies[i].start()

    barrier = pltpu.get_barrier_semaphore()
    for off in range(1, n):
        pl.semaphore_signal(
            barrier, inc=1, device_id=(grp, lax.rem(me + off, n), core), device_id_type=MESH
        )
    pl.semaphore_signal(barrier, inc=1, device_id=(grp, me, other), device_id_type=MESH)

    mine = pl.ds(pl.multiple_of(me * block, block), block)
    stage[...] = jnp.zeros_like(stage)
    for copy in small:
        copy.wait()
    held = hidden_ref[...].astype(jnp.float32)
    for h in range(2):
        for q in range(QUARTERS):
            start = h * half + q * PIECE
            stage[pl.ds(h * block + q * rows, rows), pl.ds(0, widths[q])] = held[
                :, start : start + widths[q]
            ]
    line = lax.broadcasted_iota(jnp.int32, (block, QUARTERS * total), 0)
    lane = lax.broadcasted_iota(jnp.int32, (block, QUARTERS * total), 1)
    place = jnp.zeros_like(line)
    for r in range(rows):
        place = jnp.where(line % rows == r, place_ref[r], place)
    placing = one_hot((line // rows == lane // total) & (lane % total == place))
    for h in range(2):
        first[h, mine, pl.ds(0, PIECE)] = stage[pl.ds(h * block, block), :].astype(jnp.bfloat16)
        first[h, mine, pl.ds(PIECE, QUARTERS * total)] = placing

    pl.semaphore_wait(barrier, n)

    def gather_start(step, buf, cols, chunk):
        sends = []
        for off in range(1, n):
            copy = pltpu.make_async_remote_copy(
                src_ref=buf.at[core, mine, cols],
                dst_ref=buf.at[core, mine, cols],
                send_sem=gather_send.at[step * CHUNKS + chunk, off],
                recv_sem=gather_recv.at[step * CHUNKS + chunk, off],
                device_id=(grp, lax.rem(me + off, n), core),
                device_id_type=MESH,
            )
            copy.start()
            sends.append(copy)
        return sends

    def pass_on(step, buf, off):
        slot = pl.ds(pl.multiple_of(lax.rem(me + n - off, n) * block, block), block)
        copy = pltpu.make_async_remote_copy(
            src_ref=buf.at[core, slot, :],
            dst_ref=buf.at[core, slot, :],
            send_sem=pass_send.at[step, off],
            recv_sem=pass_recv.at[step, off],
            device_id=(grp, me, other),
            device_id_type=MESH,
        )
        copy.start()
        return copy

    pending = []
    sends = [gather_start(0, first, pl.ds(0, PIECE + QUARTERS * total), 0)]
    pending += sends[0]

    for step in range(STEPS):
        ids = ids_ref[step]
        weights = weights_ref[step]
        for e in range(n):
            value = jnp.sum(jnp.where(ids == e, weights, 0.0), axis=1, keepdims=True)
            value = jnp.broadcast_to(value, (rows, 128))
            for q in range(QUARTERS):
                coef[step, e, pl.ds(q * rows, rows), :] = value
    stage[...] = jnp.zeros_like(stage)
    to = lax.broadcasted_iota(jnp.int32, (QUARTERS * total, n * block), 0)
    at = lax.broadcasted_iota(jnp.int32, (QUARTERS * total, n * block), 1)
    ordered[...] = one_hot(
        (to // total == (at // rows) % QUARTERS)
        & (to % total == (at // block) * rows + at % rows)
    )
    for copy in weight_copies[0:2] + weight_copies[3:5]:
        copy.wait()

    def half_product(buf, h, pick):
        spread = jnp.dot(pick, buf[h, :, pl.ds(0, PIECE)], preferred_element_type=jnp.float32)
        squares = jnp.sum(spread * spread, axis=1, keepdims=True)
        square = squares[0:total]
        for q in range(1, QUARTERS):
            square = square + squares[q * total : (q + 1) * total]
        scale = lax.rsqrt(square / half + epsilon)
        for q in range(QUARTERS):
            gains = [
                gain_ref[pl.ds(side * half + q * PIECE, widths[q])].reshape(1, widths[q])
                for side in range(2)
            ]
            gain = jnp.where(h == 0, gains[0], gains[1])
            piece = spread[q * total : (q + 1) * total, : widths[q]]
            normed[h, :, pl.ds(q * PIECE, widths[q])] = (piece * scale * gain).astype(jnp.bfloat16)
        gate = jnp.dot(normed[h], wg[h], preferred_element_type=jnp.float32)
        up = jnp.dot(normed[h], wu[h], preferred_element_type=jnp.float32)
        return spread, square, scale, gate, up

    current = None
    for step in range(STEPS):
        buf = first if step == 0 else second
        passes = []
        if step > 0:
            passes.append(pass_on(step, buf, 0))
        for off in range(1, n):
            for chunk in sends:
                chunk[off - 1].wait_recv()
            passes.append(pass_on(step, buf, off))
        pending += passes
        if step == 0:
            pick = jnp.transpose(
                first[core, :, pl.ds(PIECE, QUARTERS * total)].astype(jnp.float32)
            ).astype(jnp.bfloat16)
        else:
            pick = ordered[...]
        spread_own, square_own, scale_own, gate_own, up_own = half_product(buf, core, pick)
        for copy in passes:
            copy.wait_recv()
        _, square_other, scale_other, gate_other, up_other = half_product(buf, other, pick)
        scale = lax.rsqrt((square_own + square_other) / features + epsilon)
        fit_own = jnp.where(scale == 0.0, 0.0, scale / scale_own)
        fit_other = jnp.where(scale == 0.0, 0.0, scale / scale_other)
        gate = gate_own * fit_own + gate_other * fit_other
        up = up_own * fit_own + up_other * fit_other
        act = (gate / (1.0 + jnp.exp(-gate)) * up).astype(jnp.bfloat16)
        if step == 0:
            for copy in weight_copies[2::3]:
                copy.wait()
        for q in range(QUARTERS):
            cols = pl.ds(q * PIECE, widths[q])
            swap_out[step, :, cols] = jnp.dot(
                act, wd[other, :, cols], preferred_element_type=jnp.float32
            ).astype(jnp.bfloat16)
        swap = pltpu.make_async_remote_copy(
            src_ref=swap_out.at[step],
            dst_ref=swap_in.at[step],
            send_sem=swap_send.at[step],
            recv_sem=swap_recv.at[step],
            device_id=(grp, me, other),
            device_id_type=MESH,
        )
        swap.start()
        own = [
            jnp.dot(
                act, wd[core, :, pl.ds(q * PIECE, widths[q])], preferred_element_type=jnp.float32
            )
            for q in range(QUARTERS)
        ]
        if step == 0:
            to = lax.broadcasted_iota(jnp.int32, (block, QUARTERS * total), 0)
            at = lax.broadcasted_iota(jnp.int32, (block, QUARTERS * total), 1)
            keep = one_hot((to // rows == at // total) & (at % total == me * rows + to % rows))
            current = jnp.dot(
                keep, spread_own.astype(jnp.bfloat16), preferred_element_type=jnp.float32
            )
        swap.wait_recv()
        pending.append(swap)
        for q in range(QUARTERS):
            cols = pl.ds(q * PIECE, widths[q])
            value = own[q] + swap_in[step, :, cols].astype(jnp.float32)
            for p in range(n):
                stage[pl.ds(p * block + q * rows, rows), pl.ds(0, widths[q])] = value[
                    p * rows : (p + 1) * rows
                ]
        parts_out[step] = stage[...].astype(jnp.bfloat16)
        parts_in[step, mine, :] = parts_out[step, mine, :]
        width = PIECE // CHUNKS
        backs = []
        for chunk in range(CHUNKS):
            cols = pl.ds(chunk * width, width)
            for off in range(1, n):
                peer = lax.rem(me + off, n)
                slot = pl.ds(pl.multiple_of(peer * block, block), block)
                copy = pltpu.make_async_remote_copy(
                    src_ref=parts_out.at[step, slot, cols],
                    dst_ref=parts_in.at[step, mine, cols],
                    send_sem=back_send.at[step * CHUNKS + chunk, off],
                    recv_sem=back_recv.at[step * CHUNKS + chunk, off],
                    device_id=(grp, peer, core),
                    device_id_type=MESH,
                )
                copy.start()
                backs.append(copy)
        pending += backs
        results, sends = [], []
        for chunk in range(CHUNKS):
            cols = pl.ds(chunk * width, width)
            for copy in backs[chunk * (n - 1) : (chunk + 1) * (n - 1)]:
                copy.wait_recv()
            moe = None
            for e in range(n):
                value = parts_in[step, pl.ds(e * block, block), cols].astype(jnp.float32)
                value = value * jnp.concatenate([coef[step, e]] * (width // 128), axis=1)
                moe = value if moe is None else moe + value
            before = current[:, chunk * width : (chunk + 1) * width]
            piece = (before + moe).astype(jnp.bfloat16)
            results.append(piece)
            if step < STEPS - 1:
                second[core, mine, cols] = piece
                sends.append(gather_start(step + 1, second, cols, chunk))
                pending += sends[-1]
        result = jnp.concatenate(results, axis=1)
        current = result.astype(jnp.float32)

    last[core] = result
    final = pltpu.make_async_remote_copy(
        src_ref=last.at[core],
        dst_ref=last.at[core],
        send_sem=last_send,
        recv_sem=last_recv,
        device_id=(grp, me, other),
        device_id_type=MESH,
    )
    final.start()
    final.wait_recv()
    pending.append(final)
    for h in range(2):
        value = last[h].astype(jnp.float32)
        for q in range(QUARTERS):
            out_ref[:, pl.ds(h * half + q * PIECE, widths[q])] = value[
                q * rows : (q + 1) * rows, : widths[q]
            ].astype(jnp.bfloat16)
    for copy in pending:
        copy.wait_send()


def fused_shards(hidden_states, draft_row, expert_ids, route_weights, norm_gain, w_gate, w_up, w_down):
    rows, features = hidden_states.shape
    hid_dev = w_gate.shape[1]
    n = lax.axis_size("ex")
    block = QUARTERS * rows
    half = features // 2
    spread = QUARTERS * n * rows
    vmem, hbm = pl.BlockSpec(memory_space=pltpu.VMEM), pl.BlockSpec(memory_space=pltpu.HBM)
    dma = pltpu.SemaphoreType.DMA
    return pl.pallas_call(
        functools.partial(fused_kernel, n),
        out_shape=jax.ShapeDtypeStruct((rows, features), jnp.bfloat16),
        in_specs=[hbm] * 8,
        out_specs=vmem,
        scratch_shapes=[
            pltpu.VMEM((rows, features), jnp.bfloat16),
            pltpu.SMEM((rows,), jnp.int32),
            pltpu.VMEM(expert_ids.shape, jnp.int32),
            pltpu.VMEM(route_weights.shape, jnp.float32),
            pltpu.VMEM((features,), jnp.float32),
            pltpu.VMEM((2, half, hid_dev), jnp.bfloat16),
            pltpu.VMEM((2, half, hid_dev), jnp.bfloat16),
            pltpu.VMEM((2, hid_dev, half), jnp.bfloat16),
            pltpu.VMEM((2, n * block, PIECE + spread), jnp.bfloat16),
            pltpu.VMEM((2, n * block, PIECE), jnp.bfloat16),
            pltpu.VMEM((spread, n * block), jnp.bfloat16),
            pltpu.VMEM((2, n * rows, half), jnp.bfloat16),
            pltpu.VMEM((STEPS, n * rows, half), jnp.bfloat16),
            pltpu.VMEM((STEPS, n * rows, half), jnp.bfloat16),
            pltpu.VMEM((n * block, PIECE), jnp.float32),
            pltpu.VMEM((STEPS, n * block, PIECE), jnp.bfloat16),
            pltpu.VMEM((STEPS, n * block, PIECE), jnp.bfloat16),
            pltpu.VMEM((STEPS, n, block, 128), jnp.float32),
            pltpu.VMEM((2, block, PIECE), jnp.bfloat16),
            dma((5,)),
            dma((6,)),
            dma((STEPS * CHUNKS, n)),
            dma((STEPS * CHUNKS, n)),
            dma((STEPS, n)),
            dma((STEPS, n)),
            dma((STEPS,)),
            dma((STEPS,)),
            dma((STEPS * CHUNKS, n)),
            dma((STEPS * CHUNKS, n)),
            dma,
            dma,
        ],
        compiler_params=pltpu.CompilerParams(
            collective_id=0, has_side_effects=True, vmem_limit_bytes=63 * 1024 * 1024
        ),
        cost_estimate=pl.CostEstimate(
            flops=STEPS * 6 * n * rows * features * hid_dev,
            bytes_accessed=6 * features * hid_dev,
            transcendentals=STEPS * n * rows * hid_dev,
        ),
    )(
        hidden_states,
        draft_row,
        expert_ids,
        route_weights,
        norm_gain,
        w_gate,
        w_up,
        w_down,
    )


def by_size(mesh):
    def run(hidden_states, draft_row, expert_ids, route_weights, norm_gain, w_gate, w_up, w_down):
        ex = mesh.shape["ex"]
        rows = hidden_states.shape[0] // (ex * mesh.shape["grp"])
        every = expert_ids.shape[2] * HID == w_gate.shape[1]
        one_each = w_gate.shape[1] == ex * HID
        features = hidden_states.shape[1]
        shaped = (
            rows * QUARTERS == 16
            and features % 256 == 0
            and (QUARTERS - 1) * PIECE < features // 2 <= QUARTERS * PIECE
        )
        dense = every and one_each and shaped and mesh.shape["tp"] == 2
        in_specs = (
            P(("grp", "ex"), None),
            P(("grp", "ex")),
            P(None, ("grp", "ex"), None),
            P(None, ("grp", "ex"), None),
            P(),
            P(None, ("ex", "tp")),
            P(None, ("ex", "tp")),
            P(("ex", "tp"), None),
        )
        return jax.shard_map(
            fused_shards if dense else shards,
            mesh=mesh,
            in_specs=in_specs,
            out_specs=P(("grp", "ex"), None),
            check_vma=False,
        )(hidden_states, draft_row, expert_ids, route_weights, norm_gain, w_gate, w_up, w_down)

    return run


def solution(mesh):
    return by_size(mesh)
```

```python
import functools

import jax
import jax.numpy as jnp
from jax import lax
from jax.experimental import pallas as pl
from jax.experimental.pallas import tpu as pltpu
from jax.sharding import PartitionSpec as P

HID = 1024
STEPS = 2
RCAP = 2


epsilon = 1e-06


def expert_block(rows_in, w_gate, w_up, w_down):
    gate_proj = jnp.dot(rows_in, w_gate, preferred_element_type=jnp.float32)
    up_proj = jnp.dot(rows_in, w_up, preferred_element_type=jnp.float32)
    activated = (jax.nn.silu(gate_proj) * up_proj).astype(jnp.bfloat16)
    return jnp.dot(activated, w_down, preferred_element_type=jnp.float32)


def fold_back(returned, seating, route_coef, experts, group_size):
    ex_size, slot_cap, columns = returned.shape
    summed = returned.reshape(experts, group_size, slot_cap, columns).sum(axis=1)
    scale = seating.astype(jnp.float32) * route_coef.T[:, None, :]
    return jnp.einsum(
        "ecr,ecd->rd",
        scale,
        summed,
        precision=lax.Precision.HIGHEST,
        preferred_element_type=jnp.float32,
    )


def shards(hidden_states, draft_row, expert_ids, route_weights, norm_gain, w_gate, w_up, w_down):
    row_dev, features = hidden_states.shape
    ex_size = lax.axis_size("ex")
    tp_size = lax.axis_size("tp")
    hid_dev = w_gate.shape[1]
    group_size = HID // (hid_dev * tp_size)
    experts = ex_size // group_size
    chosen_count = expert_ids.shape[2]
    slot_cap = min(row_dev, max(2, 2 * row_dev * chosen_count // experts))
    target_dev = draft_row // row_dev
    target_pos = draft_row % row_dev
    same_dest = target_dev[:, None] == target_dev[None, :]
    earlier = jnp.tril(jnp.ones((row_dev, row_dev), jnp.bool_), -1)
    order_in = jnp.sum(same_dest & earlier, axis=1)
    slot_index = target_dev * RCAP + order_in
    picker = jnp.arange(ex_size * RCAP, dtype=jnp.int32)[:, None] == slot_index[None, :]
    outgoing = (
        jnp.dot(picker.astype(jnp.bfloat16), hidden_states, preferred_element_type=jnp.float32)
        .astype(jnp.bfloat16)
        .reshape(ex_size, RCAP, features)
    )
    labels = (
        jnp.sum(jnp.where(picker, target_pos[None, :] + 1, 0), axis=1)
        .astype(jnp.bfloat16)
        .reshape(ex_size, RCAP)
    )
    arrived, arrived_labels = (
        lax.all_to_all(outgoing, "ex", split_axis=0, concat_axis=0, tiled=True),
        lax.all_to_all(labels, "ex", split_axis=0, concat_axis=0, tiled=True),
    )
    arrived = arrived.reshape(ex_size * RCAP, features)
    settle = (
        arrived_labels.reshape(-1).astype(jnp.float32)[None, :]
        == (jnp.arange(row_dev) + 1).astype(jnp.float32)[:, None]
    )
    current = jnp.dot(
        settle.astype(jnp.bfloat16), arrived, preferred_element_type=jnp.float32
    ).astype(jnp.bfloat16)
    slot_total = ex_size * slot_cap
    for step_no in range(STEPS):
        as_float = current.astype(jnp.float32)
        mean_square = jnp.mean(as_float * as_float, axis=-1, keepdims=True)
        normed = (as_float * lax.rsqrt(mean_square + epsilon) * norm_gain).astype(jnp.bfloat16)
        step_ids = expert_ids[step_no]
        weights = route_weights[step_no]
        matches = step_ids[:, :, None] == jnp.arange(experts, dtype=jnp.int32)[None, None, :]
        chosen = jnp.any(matches, axis=1)
        route_coef = jnp.sum(jnp.where(matches, weights[:, :, None], 0.0), axis=1)
        chosen_int = chosen.astype(jnp.int32)
        before = jnp.cumsum(chosen_int, axis=0) - chosen_int
        seating = chosen.T[:, None, :] & (
            before.T[:, None, :] == jnp.arange(slot_cap, dtype=jnp.int32)[None, :, None]
        )
        packed_base = jnp.einsum(
            "ecr,rd->ecd", seating.astype(jnp.bfloat16), normed, preferred_element_type=jnp.float32
        ).astype(jnp.bfloat16)
        occupancy = jnp.any(seating, axis=2).astype(jnp.bfloat16)
        occupancy = jnp.broadcast_to(occupancy[:, None], (experts, group_size, slot_cap)).reshape(
            ex_size, slot_cap
        )
        packed = jnp.broadcast_to(
            packed_base[:, None], (experts, group_size, slot_cap, features)
        ).reshape(ex_size, slot_cap, features)
        landed, landed_flags = (
            lax.all_to_all(packed, "ex", split_axis=0, concat_axis=0, tiled=True),
            lax.all_to_all(occupancy, "ex", split_axis=0, concat_axis=0, tiled=True),
        )
        rows_in = landed.reshape(slot_total, features)
        partial_value = expert_block(rows_in, w_gate, w_up, w_down)
        returned = lax.all_to_all(
            partial_value.reshape(ex_size, slot_cap, features).astype(jnp.bfloat16),
            "ex",
            split_axis=0,
            concat_axis=0,
            tiled=True,
        ).astype(jnp.float32)
        branch_sum = lax.psum(
            fold_back(returned, seating, route_coef, experts, group_size).astype(jnp.bfloat16), "tp"
        ).astype(jnp.float32)
        current = (current.astype(jnp.float32) + branch_sum).astype(jnp.bfloat16)
    return current


QUARTERS = 4
PIECE = 512
MESH = pl.DeviceIdType.MESH


def one_hot(condition, dtype=jnp.bfloat16):
    return jnp.where(condition, 1.0, 0.0).astype(dtype)


def fused_kernel(
    n,
    hidden_hbm,
    place_hbm,
    ids_hbm,
    weights_hbm,
    gain_hbm,
    wg_hbm,
    wu_hbm,
    wd_hbm,
    out_ref,
    hidden_ref,
    place_ref,
    ids_ref,
    weights_ref,
    gain_ref,
    wg,
    wu,
    wd,
    first,
    second,
    ordered,
    normed,
    swap_out,
    swap_in,
    stage,
    parts_out,
    parts_in,
    coef,
    last,
    small_sem,
    weight_sem,
    gather_send,
    gather_recv,
    pass_send,
    pass_recv,
    swap_send,
    swap_recv,
    back_send,
    back_recv,
    last_send,
    last_recv,
):
    rows, features = hidden_ref.shape
    half = features // 2
    block = QUARTERS * rows
    total = n * rows
    widths = [min(PIECE, half - q * PIECE) for q in range(QUARTERS)]
    grp, me, core = lax.axis_index("grp"), lax.axis_index("ex"), lax.axis_index("tp")
    other = 1 - core

    def partner(off):
        index, digit = 0, 1
        while digit < n:
            own = lax.rem(me // digit, 2)
            index = index + (1 - own if off // digit % 2 else own) * digit
            digit *= 2
        return index

    turns = sorted(range(1, n), key=lambda off: (off >= n // 2, off % 2, off), reverse=True)

    small = [
        pltpu.make_async_copy(source, target, small_sem.at[i])
        for i, (source, target) in enumerate(
            (
                (hidden_hbm, hidden_ref),
                (place_hbm, place_ref),
                (ids_hbm, ids_ref),
                (weights_hbm, weights_ref),
                (gain_hbm, gain_ref),
            )
        )
    ]
    for copy in small:
        copy.start()
    weight_copies = []
    for h in range(2):
        span = pl.ds(h * half, half)
        for which, (source, target) in enumerate(
            (
                (wg_hbm.at[span, :], wg.at[h]),
                (wu_hbm.at[span, :], wu.at[h]),
                (wd_hbm.at[:, span], wd.at[h]),
            )
        ):
            weight_copies.append(
                pltpu.make_async_copy(source, target, weight_sem.at[h * 3 + which])
            )
    for i in (0, 3, 1, 4, 2, 5):
        weight_copies[i].start()

    barrier = pltpu.get_barrier_semaphore()
    for off in turns:
        pl.semaphore_signal(
            barrier, inc=1, device_id=(grp, partner(off), core), device_id_type=MESH
        )
    pl.semaphore_signal(barrier, inc=1, device_id=(grp, me, other), device_id_type=MESH)

    mine = pl.ds(pl.multiple_of(me * block, block), block)
    stage[...] = jnp.zeros_like(stage)
    for copy in small:
        copy.wait()
    held = hidden_ref[...].astype(jnp.float32)
    for h in range(2):
        for q in range(QUARTERS):
            start = h * half + q * PIECE
            stage[pl.ds(h * block + q * rows, rows), pl.ds(0, widths[q])] = held[
                :, start : start + widths[q]
            ]
    line = lax.broadcasted_iota(jnp.int32, (block, QUARTERS * total), 0)
    lane = lax.broadcasted_iota(jnp.int32, (block, QUARTERS * total), 1)
    place = jnp.zeros_like(line)
    for r in range(rows):
        place = jnp.where(line % rows == r, place_ref[r], place)
    placing = one_hot((line // rows == lane // total) & (lane % total == place))
    for h in range(2):
        first[h, mine, pl.ds(0, PIECE)] = stage[pl.ds(h * block, block), :].astype(jnp.bfloat16)
        first[h, mine, pl.ds(PIECE, QUARTERS * total)] = placing

    pl.semaphore_wait(barrier, n)

    def gather_start(step, buf):
        sends = []
        for off in turns:
            copy = pltpu.make_async_remote_copy(
                src_ref=buf.at[core, mine, :],
                dst_ref=buf.at[core, mine, :],
                send_sem=gather_send.at[step, off],
                recv_sem=gather_recv.at[step, off],
                device_id=(grp, partner(off), core),
                device_id_type=MESH,
            )
            copy.start()
            sends.append(copy)
        return sends

    def pass_on(step, buf, off):
        slot = pl.ds(pl.multiple_of((partner(off) if off else me) * block, block), block)
        copy = pltpu.make_async_remote_copy(
            src_ref=buf.at[core, slot, :],
            dst_ref=buf.at[core, slot, :],
            send_sem=pass_send.at[step, off],
            recv_sem=pass_recv.at[step, off],
            device_id=(grp, me, other),
            device_id_type=MESH,
        )
        copy.start()
        return copy

    pending = []
    sends = gather_start(0, first)
    pending += sends

    for step in range(STEPS):
        ids = ids_ref[step]
        weights = weights_ref[step]
        for e in range(n):
            value = jnp.sum(jnp.where(ids == e, weights, 0.0), axis=1, keepdims=True)
            value = jnp.broadcast_to(value, (rows, 128))
            for q in range(QUARTERS):
                coef[step, e, pl.ds(q * rows, rows), :] = value
    stage[...] = jnp.zeros_like(stage)
    to = lax.broadcasted_iota(jnp.int32, (QUARTERS * total, n * block), 0)
    at = lax.broadcasted_iota(jnp.int32, (QUARTERS * total, n * block), 1)
    ordered[...] = one_hot(
        (to // total == (at // rows) % QUARTERS)
        & (to % total == (at // block) * rows + at % rows)
    )
    for copy in weight_copies[0:2] + weight_copies[3:5]:
        copy.wait()

    def half_product(buf, h, pick):
        spread = jnp.dot(pick, buf[h, :, pl.ds(0, PIECE)], preferred_element_type=jnp.float32)
        squares = jnp.sum(spread * spread, axis=1, keepdims=True)
        square = squares[0:total]
        for q in range(1, QUARTERS):
            square = square + squares[q * total : (q + 1) * total]
        scale = lax.rsqrt(square / half + epsilon)
        for q in range(QUARTERS):
            gains = [
                gain_ref[pl.ds(side * half + q * PIECE, widths[q])].reshape(1, widths[q])
                for side in range(2)
            ]
            gain = jnp.where(h == 0, gains[0], gains[1])
            piece = spread[q * total : (q + 1) * total, : widths[q]]
            normed[h, :, pl.ds(q * PIECE, widths[q])] = (piece * scale * gain).astype(jnp.bfloat16)
        gate = jnp.dot(normed[h], wg[h], preferred_element_type=jnp.float32)
        up = jnp.dot(normed[h], wu[h], preferred_element_type=jnp.float32)
        return spread, square, scale, gate, up

    current = None
    for step in range(STEPS):
        buf = first if step == 0 else second
        passes = []
        if step > 0:
            passes.append(pass_on(step, buf, 0))
        for off in turns:
            sends[turns.index(off)].wait_recv()
            passes.append(pass_on(step, buf, off))
        pending += passes
        if step == 0:
            pick = jnp.transpose(
                first[core, :, pl.ds(PIECE, QUARTERS * total)].astype(jnp.float32)
            ).astype(jnp.bfloat16)
        else:
            pick = ordered[...]
        spread_own, square_own, scale_own, gate_own, up_own = half_product(buf, core, pick)
        for copy in passes:
            copy.wait_recv()
        _, square_other, scale_other, gate_other, up_other = half_product(buf, other, pick)
        scale = lax.rsqrt((square_own + square_other) / features + epsilon)
        fit_own = jnp.where(scale == 0.0, 0.0, scale / scale_own)
        fit_other = jnp.where(scale == 0.0, 0.0, scale / scale_other)
        gate = gate_own * fit_own + gate_other * fit_other
        up = up_own * fit_own + up_other * fit_other
        act = (gate / (1.0 + jnp.exp(-gate)) * up).astype(jnp.bfloat16)
        if step == 0:
            for copy in weight_copies[2::3]:
                copy.wait()
        for q in range(QUARTERS):
            cols = pl.ds(q * PIECE, widths[q])
            swap_out[step, :, cols] = jnp.dot(
                act, wd[other, :, cols], preferred_element_type=jnp.float32
            ).astype(jnp.bfloat16)
        swap = pltpu.make_async_remote_copy(
            src_ref=swap_out.at[step],
            dst_ref=swap_in.at[step],
            send_sem=swap_send.at[step],
            recv_sem=swap_recv.at[step],
            device_id=(grp, me, other),
            device_id_type=MESH,
        )
        swap.start()
        own = [
            jnp.dot(
                act, wd[core, :, pl.ds(q * PIECE, widths[q])], preferred_element_type=jnp.float32
            )
            for q in range(QUARTERS)
        ]
        if step == 0:
            to = lax.broadcasted_iota(jnp.int32, (block, QUARTERS * total), 0)
            at = lax.broadcasted_iota(jnp.int32, (block, QUARTERS * total), 1)
            keep = one_hot((to // rows == at // total) & (at % total == me * rows + to % rows))
            current = jnp.dot(
                keep, spread_own.astype(jnp.bfloat16), preferred_element_type=jnp.float32
            )
        swap.wait_recv()
        pending.append(swap)
        for q in range(QUARTERS):
            cols = pl.ds(q * PIECE, widths[q])
            value = own[q] + swap_in[step, :, cols].astype(jnp.float32)
            for p in range(n):
                stage[pl.ds(p * block + q * rows, rows), pl.ds(0, widths[q])] = value[
                    p * rows : (p + 1) * rows
                ]
        parts_out[step] = stage[...].astype(jnp.bfloat16)
        backs = []
        for off in turns:
            peer = partner(off)
            copy = pltpu.make_async_remote_copy(
                src_ref=parts_out.at[step, pl.ds(pl.multiple_of(peer * block, block), block), :],
                dst_ref=parts_in.at[step, mine, :],
                send_sem=back_send.at[step, off],
                recv_sem=back_recv.at[step, off],
                device_id=(grp, peer, core),
                device_id_type=MESH,
            )
            copy.start()
            backs.append(copy)
        parts_in[step, mine, :] = parts_out[step, mine, :]
        for copy in backs:
            copy.wait_recv()
        pending += backs
        moe = None
        for e in range(n):
            value = parts_in[step, pl.ds(e * block, block), :].astype(jnp.float32)
            value = value * jnp.concatenate([coef[step, e]] * (PIECE // 128), axis=1)
            moe = value if moe is None else moe + value
        result = (current + moe).astype(jnp.bfloat16)
        current = result.astype(jnp.float32)
        if step < STEPS - 1:
            second[core, mine, :] = result
            sends = gather_start(step + 1, second)
            pending += sends

    last[core] = result
    final = pltpu.make_async_remote_copy(
        src_ref=last.at[core],
        dst_ref=last.at[core],
        send_sem=last_send,
        recv_sem=last_recv,
        device_id=(grp, me, other),
        device_id_type=MESH,
    )
    final.start()
    final.wait_recv()
    pending.append(final)
    for h in range(2):
        value = last[h].astype(jnp.float32)
        for q in range(QUARTERS):
            out_ref[:, pl.ds(h * half + q * PIECE, widths[q])] = value[
                q * rows : (q + 1) * rows, : widths[q]
            ].astype(jnp.bfloat16)
    for copy in pending:
        copy.wait_send()


def fused_shards(hidden_states, draft_row, expert_ids, route_weights, norm_gain, w_gate, w_up, w_down):
    rows, features = hidden_states.shape
    hid_dev = w_gate.shape[1]
    n = lax.axis_size("ex")
    block = QUARTERS * rows
    half = features // 2
    spread = QUARTERS * n * rows
    vmem, hbm = pl.BlockSpec(memory_space=pltpu.VMEM), pl.BlockSpec(memory_space=pltpu.HBM)
    dma = pltpu.SemaphoreType.DMA
    return pl.pallas_call(
        functools.partial(fused_kernel, n),
        out_shape=jax.ShapeDtypeStruct((rows, features), jnp.bfloat16),
        in_specs=[hbm] * 8,
        out_specs=vmem,
        scratch_shapes=[
            pltpu.VMEM((rows, features), jnp.bfloat16),
            pltpu.SMEM((rows,), jnp.int32),
            pltpu.VMEM(expert_ids.shape, jnp.int32),
            pltpu.VMEM(route_weights.shape, jnp.float32),
            pltpu.VMEM((features,), jnp.float32),
            pltpu.VMEM((2, half, hid_dev), jnp.bfloat16),
            pltpu.VMEM((2, half, hid_dev), jnp.bfloat16),
            pltpu.VMEM((2, hid_dev, half), jnp.bfloat16),
            pltpu.VMEM((2, n * block, PIECE + spread), jnp.bfloat16),
            pltpu.VMEM((2, n * block, PIECE), jnp.bfloat16),
            pltpu.VMEM((spread, n * block), jnp.bfloat16),
            pltpu.VMEM((2, n * rows, half), jnp.bfloat16),
            pltpu.VMEM((STEPS, n * rows, half), jnp.bfloat16),
            pltpu.VMEM((STEPS, n * rows, half), jnp.bfloat16),
            pltpu.VMEM((n * block, PIECE), jnp.float32),
            pltpu.VMEM((STEPS, n * block, PIECE), jnp.bfloat16),
            pltpu.VMEM((STEPS, n * block, PIECE), jnp.bfloat16),
            pltpu.VMEM((STEPS, n, block, 128), jnp.float32),
            pltpu.VMEM((2, block, PIECE), jnp.bfloat16),
            dma((5,)),
            dma((6,)),
            dma((STEPS, n)),
            dma((STEPS, n)),
            dma((STEPS, n)),
            dma((STEPS, n)),
            dma((STEPS,)),
            dma((STEPS,)),
            dma((STEPS, n)),
            dma((STEPS, n)),
            dma,
            dma,
        ],
        compiler_params=pltpu.CompilerParams(
            collective_id=0, has_side_effects=True, vmem_limit_bytes=63 * 1024 * 1024
        ),
        cost_estimate=pl.CostEstimate(
            flops=STEPS * 6 * n * rows * features * hid_dev,
            bytes_accessed=6 * features * hid_dev,
            transcendentals=STEPS * n * rows * hid_dev,
        ),
    )(
        hidden_states,
        draft_row,
        expert_ids,
        route_weights,
        norm_gain,
        w_gate,
        w_up,
        w_down,
    )


def by_size(mesh):
    def run(hidden_states, draft_row, expert_ids, route_weights, norm_gain, w_gate, w_up, w_down):
        ex = mesh.shape["ex"]
        rows = hidden_states.shape[0] // (ex * mesh.shape["grp"])
        every = expert_ids.shape[2] * HID == w_gate.shape[1]
        one_each = w_gate.shape[1] == ex * HID
        features = hidden_states.shape[1]
        shaped = (
            rows * QUARTERS == 16
            and features % 256 == 0
            and (QUARTERS - 1) * PIECE < features // 2 <= QUARTERS * PIECE
        )
        ex_power = ex & (ex - 1) == 0
        dense = ex_power and every and one_each and shaped and mesh.shape["tp"] == 2
        in_specs = (
            P(("grp", "ex"), None),
            P(("grp", "ex")),
            P(None, ("grp", "ex"), None),
            P(None, ("grp", "ex"), None),
            P(),
            P(None, ("ex", "tp")),
            P(None, ("ex", "tp")),
            P(("ex", "tp"), None),
        )
        return jax.shard_map(
            fused_shards if dense else shards,
            mesh=mesh,
            in_specs=in_specs,
            out_specs=P(("grp", "ex"), None),
            check_vma=False,
        )(hidden_states, draft_row, expert_ids, route_weights, norm_gain, w_gate, w_up, w_down)

    return run


def solution(mesh):
    return by_size(mesh)
```

```python
import functools

import jax
import jax.numpy as jnp
from jax import lax
from jax.experimental import pallas as pl
from jax.experimental.pallas import tpu as pltpu
from jax.sharding import PartitionSpec as P

HID = 1024
STEPS = 2
RCAP = 2


epsilon = 1e-06


def expert_block(rows_in, w_gate, w_up, w_down):
    gate_proj = jnp.dot(rows_in, w_gate, preferred_element_type=jnp.float32)
    up_proj = jnp.dot(rows_in, w_up, preferred_element_type=jnp.float32)
    activated = (jax.nn.silu(gate_proj) * up_proj).astype(jnp.bfloat16)
    return jnp.dot(activated, w_down, preferred_element_type=jnp.float32)


def fold_back(returned, seating, route_coef, experts, group_size):
    ex_size, slot_cap, columns = returned.shape
    summed = returned.reshape(experts, group_size, slot_cap, columns).sum(axis=1)
    scale = seating.astype(jnp.float32) * route_coef.T[:, None, :]
    return jnp.einsum(
        "ecr,ecd->rd",
        scale,
        summed,
        precision=lax.Precision.HIGHEST,
        preferred_element_type=jnp.float32,
    )


def shards(hidden_states, draft_row, expert_ids, route_weights, norm_gain, w_gate, w_up, w_down):
    row_dev, features = hidden_states.shape
    ex_size = lax.axis_size("ex")
    tp_size = lax.axis_size("tp")
    hid_dev = w_gate.shape[1]
    group_size = HID // (hid_dev * tp_size)
    experts = ex_size // group_size
    chosen_count = expert_ids.shape[2]
    slot_cap = min(row_dev, max(2, 2 * row_dev * chosen_count // experts))
    target_dev = draft_row // row_dev
    target_pos = draft_row % row_dev
    same_dest = target_dev[:, None] == target_dev[None, :]
    earlier = jnp.tril(jnp.ones((row_dev, row_dev), jnp.bool_), -1)
    order_in = jnp.sum(same_dest & earlier, axis=1)
    slot_index = target_dev * RCAP + order_in
    picker = jnp.arange(ex_size * RCAP, dtype=jnp.int32)[:, None] == slot_index[None, :]
    outgoing = (
        jnp.dot(picker.astype(jnp.bfloat16), hidden_states, preferred_element_type=jnp.float32)
        .astype(jnp.bfloat16)
        .reshape(ex_size, RCAP, features)
    )
    labels = (
        jnp.sum(jnp.where(picker, target_pos[None, :] + 1, 0), axis=1)
        .astype(jnp.bfloat16)
        .reshape(ex_size, RCAP)
    )
    arrived, arrived_labels = (
        lax.all_to_all(outgoing, "ex", split_axis=0, concat_axis=0, tiled=True),
        lax.all_to_all(labels, "ex", split_axis=0, concat_axis=0, tiled=True),
    )
    arrived = arrived.reshape(ex_size * RCAP, features)
    settle = (
        arrived_labels.reshape(-1).astype(jnp.float32)[None, :]
        == (jnp.arange(row_dev) + 1).astype(jnp.float32)[:, None]
    )
    current = jnp.dot(
        settle.astype(jnp.bfloat16), arrived, preferred_element_type=jnp.float32
    ).astype(jnp.bfloat16)
    slot_total = ex_size * slot_cap
    for step_no in range(STEPS):
        as_float = current.astype(jnp.float32)
        mean_square = jnp.mean(as_float * as_float, axis=-1, keepdims=True)
        normed = (as_float * lax.rsqrt(mean_square + epsilon) * norm_gain).astype(jnp.bfloat16)
        step_ids = expert_ids[step_no]
        weights = route_weights[step_no]
        matches = step_ids[:, :, None] == jnp.arange(experts, dtype=jnp.int32)[None, None, :]
        chosen = jnp.any(matches, axis=1)
        route_coef = jnp.sum(jnp.where(matches, weights[:, :, None], 0.0), axis=1)
        chosen_int = chosen.astype(jnp.int32)
        before = jnp.cumsum(chosen_int, axis=0) - chosen_int
        seating = chosen.T[:, None, :] & (
            before.T[:, None, :] == jnp.arange(slot_cap, dtype=jnp.int32)[None, :, None]
        )
        packed_base = jnp.einsum(
            "ecr,rd->ecd", seating.astype(jnp.bfloat16), normed, preferred_element_type=jnp.float32
        ).astype(jnp.bfloat16)
        occupancy = jnp.any(seating, axis=2).astype(jnp.bfloat16)
        occupancy = jnp.broadcast_to(occupancy[:, None], (experts, group_size, slot_cap)).reshape(
            ex_size, slot_cap
        )
        packed = jnp.broadcast_to(
            packed_base[:, None], (experts, group_size, slot_cap, features)
        ).reshape(ex_size, slot_cap, features)
        landed, landed_flags = (
            lax.all_to_all(packed, "ex", split_axis=0, concat_axis=0, tiled=True),
            lax.all_to_all(occupancy, "ex", split_axis=0, concat_axis=0, tiled=True),
        )
        rows_in = landed.reshape(slot_total, features)
        partial_value = expert_block(rows_in, w_gate, w_up, w_down)
        returned = lax.all_to_all(
            partial_value.reshape(ex_size, slot_cap, features).astype(jnp.bfloat16),
            "ex",
            split_axis=0,
            concat_axis=0,
            tiled=True,
        ).astype(jnp.float32)
        branch_sum = lax.psum(
            fold_back(returned, seating, route_coef, experts, group_size).astype(jnp.bfloat16), "tp"
        ).astype(jnp.float32)
        current = (current.astype(jnp.float32) + branch_sum).astype(jnp.bfloat16)
    return current


QUARTERS = 4
PIECE = 512
MESH = pl.DeviceIdType.MESH


def one_hot(condition, dtype=jnp.bfloat16):
    return jnp.where(condition, 1.0, 0.0).astype(dtype)


def fused_kernel(
    n,
    hidden_hbm,
    place_hbm,
    ids_hbm,
    weights_hbm,
    gain_hbm,
    wg_hbm,
    wu_hbm,
    wd_hbm,
    out_ref,
    hidden_ref,
    place_ref,
    ids_ref,
    weights_ref,
    gain_ref,
    wg,
    wu,
    wd,
    first,
    second,
    ordered,
    normed,
    swap_out,
    swap_in,
    stage,
    parts_out,
    parts_in,
    coef,
    last,
    small_sem,
    weight_sem,
    gather_send,
    gather_recv,
    pass_send,
    pass_recv,
    swap_send,
    swap_recv,
    back_send,
    back_recv,
    last_send,
    last_recv,
):
    rows, features = hidden_ref.shape
    half = features // 2
    block = QUARTERS * rows
    total = n * rows
    widths = [min(PIECE, half - q * PIECE) for q in range(QUARTERS)]
    grp, me, core = lax.axis_index("grp"), lax.axis_index("ex"), lax.axis_index("tp")
    other = 1 - core

    small = [
        pltpu.make_async_copy(source, target, small_sem.at[i])
        for i, (source, target) in enumerate(
            (
                (hidden_hbm, hidden_ref),
                (place_hbm, place_ref),
                (ids_hbm, ids_ref),
                (weights_hbm, weights_ref),
                (gain_hbm, gain_ref),
            )
        )
    ]
    for copy in small:
        copy.start()
    barrier = pltpu.get_barrier_semaphore()
    for off in range(1, n):
        pl.semaphore_signal(
            barrier, inc=1, device_id=(grp, lax.rem(me + off, n), core), device_id_type=MESH
        )
    pl.semaphore_signal(barrier, inc=1, device_id=(grp, me, other), device_id_type=MESH)

    weight_copies = []
    for h in range(2):
        span = pl.ds(h * half, half)
        for which, (source, target) in enumerate(
            (
                (wg_hbm.at[span, :], wg.at[h]),
                (wu_hbm.at[span, :], wu.at[h]),
                (wd_hbm.at[:, span], wd.at[h]),
            )
        ):
            weight_copies.append(
                pltpu.make_async_copy(source, target, weight_sem.at[h * 3 + which])
            )
    for i in (0, 3, 1, 4, 2, 5):
        weight_copies[i].start()

    mine = pl.ds(pl.multiple_of(me * block, block), block)
    stage[...] = jnp.zeros_like(stage)
    for copy in small:
        copy.wait()
    held = hidden_ref[...].astype(jnp.float32)
    for h in range(2):
        for q in range(QUARTERS):
            start = h * half + q * PIECE
            stage[pl.ds(h * block + q * rows, rows), pl.ds(0, widths[q])] = held[
                :, start : start + widths[q]
            ]
    line = lax.broadcasted_iota(jnp.int32, (block, QUARTERS * total), 0)
    lane = lax.broadcasted_iota(jnp.int32, (block, QUARTERS * total), 1)
    place = jnp.zeros_like(line)
    for r in range(rows):
        place = jnp.where(line % rows == r, place_ref[r], place)
    placing = one_hot((line // rows == lane // total) & (lane % total == place))
    for h in range(2):
        first[h, mine, pl.ds(0, PIECE)] = stage[pl.ds(h * block, block), :].astype(jnp.bfloat16)
        first[h, mine, pl.ds(PIECE, QUARTERS * total)] = placing

    pl.semaphore_wait(barrier, n)

    def gather_start(step, buf):
        sends = []
        for off in range(1, n):
            copy = pltpu.make_async_remote_copy(
                src_ref=buf.at[core, mine, :],
                dst_ref=buf.at[core, mine, :],
                send_sem=gather_send.at[step, off],
                recv_sem=gather_recv.at[step, off],
                device_id=(grp, lax.rem(me + off, n), core),
                device_id_type=MESH,
            )
            copy.start()
            sends.append(copy)
        return sends

    def pass_on(step, buf, off):
        slot = pl.ds(pl.multiple_of(lax.rem(me + n - off, n) * block, block), block)
        copy = pltpu.make_async_remote_copy(
            src_ref=buf.at[core, slot, :],
            dst_ref=buf.at[core, slot, :],
            send_sem=pass_send.at[step, off],
            recv_sem=pass_recv.at[step, off],
            device_id=(grp, me, other),
            device_id_type=MESH,
        )
        copy.start()
        return copy

    pending = []
    sends = gather_start(0, first)
    pending += sends

    for step in range(STEPS):
        ids = ids_ref[step]
        weights = weights_ref[step]
        for e in range(n):
            value = jnp.sum(jnp.where(ids == e, weights, 0.0), axis=1, keepdims=True)
            value = jnp.broadcast_to(value, (rows, 128))
            for q in range(QUARTERS):
                coef[step, e, pl.ds(q * rows, rows), :] = value
    stage[...] = jnp.zeros_like(stage)
    to = lax.broadcasted_iota(jnp.int32, (QUARTERS * total, n * block), 0)
    at = lax.broadcasted_iota(jnp.int32, (QUARTERS * total, n * block), 1)
    ordered[...] = one_hot(
        (to // total == (at // rows) % QUARTERS)
        & (to % total == (at // block) * rows + at % rows)
    )
    for copy in weight_copies[0:2] + weight_copies[3:5]:
        copy.wait()

    def half_product(buf, h, pick):
        spread = jnp.dot(pick, buf[h, :, pl.ds(0, PIECE)], preferred_element_type=jnp.float32)
        squares = jnp.sum(spread * spread, axis=1, keepdims=True)
        square = squares[0:total]
        for q in range(1, QUARTERS):
            square = square + squares[q * total : (q + 1) * total]
        scale = lax.rsqrt(square / half + epsilon)
        for q in range(QUARTERS):
            gains = [
                gain_ref[pl.ds(side * half + q * PIECE, widths[q])].reshape(1, widths[q])
                for side in range(2)
            ]
            gain = jnp.where(h == 0, gains[0], gains[1])
            piece = spread[q * total : (q + 1) * total, : widths[q]]
            normed[h, :, pl.ds(q * PIECE, widths[q])] = (piece * scale * gain).astype(jnp.bfloat16)
        gate = jnp.dot(normed[h], wg[h], preferred_element_type=jnp.float32)
        up = jnp.dot(normed[h], wu[h], preferred_element_type=jnp.float32)
        return spread, square, scale, gate, up

    current = None
    for step in range(STEPS):
        buf = first if step == 0 else second
        passes = []
        if step > 0:
            passes.append(pass_on(step, buf, 0))
        for off in range(1, n):
            sends[off - 1].wait_recv()
            passes.append(pass_on(step, buf, off))
        pending += passes
        if step == 0:
            pick = jnp.transpose(
                first[core, :, pl.ds(PIECE, QUARTERS * total)].astype(jnp.float32)
            ).astype(jnp.bfloat16)
        else:
            pick = ordered[...]
        spread_own, square_own, scale_own, gate_own, up_own = half_product(buf, core, pick)
        for copy in passes:
            copy.wait_recv()
        _, square_other, scale_other, gate_other, up_other = half_product(buf, other, pick)
        scale = lax.rsqrt((square_own + square_other) / features + epsilon)
        fit_own = jnp.where(scale == 0.0, 0.0, scale / scale_own)
        fit_other = jnp.where(scale == 0.0, 0.0, scale / scale_other)
        gate = gate_own * fit_own + gate_other * fit_other
        up = up_own * fit_own + up_other * fit_other
        act = (gate / (1.0 + jnp.exp(-gate)) * up).astype(jnp.bfloat16)
        if step == 0:
            for copy in weight_copies[2::3]:
                copy.wait()
        for q in range(QUARTERS):
            cols = pl.ds(q * PIECE, widths[q])
            swap_out[step, :, cols] = jnp.dot(
                act, wd[other, :, cols], preferred_element_type=jnp.float32
            ).astype(jnp.bfloat16)
        swap = pltpu.make_async_remote_copy(
            src_ref=swap_out.at[step],
            dst_ref=swap_in.at[step],
            send_sem=swap_send.at[step],
            recv_sem=swap_recv.at[step],
            device_id=(grp, me, other),
            device_id_type=MESH,
        )
        swap.start()
        own = [
            jnp.dot(
                act, wd[core, :, pl.ds(q * PIECE, widths[q])], preferred_element_type=jnp.float32
            )
            for q in range(QUARTERS)
        ]
        if step == 0:
            to = lax.broadcasted_iota(jnp.int32, (block, QUARTERS * total), 0)
            at = lax.broadcasted_iota(jnp.int32, (block, QUARTERS * total), 1)
            keep = one_hot((to // rows == at // total) & (at % total == me * rows + to % rows))
            current = jnp.dot(
                keep, spread_own.astype(jnp.bfloat16), preferred_element_type=jnp.float32
            )
        swap.wait_recv()
        pending.append(swap)
        for q in range(QUARTERS):
            cols = pl.ds(q * PIECE, widths[q])
            value = own[q] + swap_in[step, :, cols].astype(jnp.float32)
            for p in range(n):
                stage[pl.ds(p * block + q * rows, rows), pl.ds(0, widths[q])] = value[
                    p * rows : (p + 1) * rows
                ]
        parts_out[step] = stage[...].astype(jnp.bfloat16)
        backs = []
        for off in range(1, n):
            peer = lax.rem(me + off, n)
            copy = pltpu.make_async_remote_copy(
                src_ref=parts_out.at[step, pl.ds(pl.multiple_of(peer * block, block), block), :],
                dst_ref=parts_in.at[step, mine, :],
                send_sem=back_send.at[step, off],
                recv_sem=back_recv.at[step, off],
                device_id=(grp, peer, core),
                device_id_type=MESH,
            )
            copy.start()
            backs.append(copy)
        parts_in[step, mine, :] = parts_out[step, mine, :]
        for copy in backs:
            copy.wait_recv()
        pending += backs
        moe = None
        for e in range(n):
            value = parts_in[step, pl.ds(e * block, block), :].astype(jnp.float32)
            value = value * jnp.concatenate([coef[step, e]] * (PIECE // 128), axis=1)
            moe = value if moe is None else moe + value
        result = (current + moe).astype(jnp.bfloat16)
        current = result.astype(jnp.float32)
        if step < STEPS - 1:
            second[core, mine, :] = result
            sends = gather_start(step + 1, second)
            pending += sends

    last[core] = result
    final = pltpu.make_async_remote_copy(
        src_ref=last.at[core],
        dst_ref=last.at[core],
        send_sem=last_send,
        recv_sem=last_recv,
        device_id=(grp, me, other),
        device_id_type=MESH,
    )
    final.start()
    final.wait_recv()
    pending.append(final)
    for h in range(2):
        value = last[h].astype(jnp.float32)
        for q in range(QUARTERS):
            out_ref[:, pl.ds(h * half + q * PIECE, widths[q])] = value[
                q * rows : (q + 1) * rows, : widths[q]
            ].astype(jnp.bfloat16)
    for copy in pending:
        copy.wait_send()


def fused_shards(hidden_states, draft_row, expert_ids, route_weights, norm_gain, w_gate, w_up, w_down):
    rows, features = hidden_states.shape
    hid_dev = w_gate.shape[1]
    n = lax.axis_size("ex")
    block = QUARTERS * rows
    half = features // 2
    spread = QUARTERS * n * rows
    vmem, hbm = pl.BlockSpec(memory_space=pltpu.VMEM), pl.BlockSpec(memory_space=pltpu.HBM)
    dma = pltpu.SemaphoreType.DMA
    return pl.pallas_call(
        functools.partial(fused_kernel, n),
        out_shape=jax.ShapeDtypeStruct((rows, features), jnp.bfloat16),
        in_specs=[hbm] * 8,
        out_specs=vmem,
        scratch_shapes=[
            pltpu.VMEM((rows, features), jnp.bfloat16),
            pltpu.SMEM((rows,), jnp.int32),
            pltpu.VMEM(expert_ids.shape, jnp.int32),
            pltpu.VMEM(route_weights.shape, jnp.float32),
            pltpu.VMEM((features,), jnp.float32),
            pltpu.VMEM((2, half, hid_dev), jnp.bfloat16),
            pltpu.VMEM((2, half, hid_dev), jnp.bfloat16),
            pltpu.VMEM((2, hid_dev, half), jnp.bfloat16),
            pltpu.VMEM((2, n * block, PIECE + spread), jnp.bfloat16),
            pltpu.VMEM((2, n * block, PIECE), jnp.bfloat16),
            pltpu.VMEM((spread, n * block), jnp.bfloat16),
            pltpu.VMEM((2, n * rows, half), jnp.bfloat16),
            pltpu.VMEM((STEPS, n * rows, half), jnp.bfloat16),
            pltpu.VMEM((STEPS, n * rows, half), jnp.bfloat16),
            pltpu.VMEM((n * block, PIECE), jnp.float32),
            pltpu.VMEM((STEPS, n * block, PIECE), jnp.bfloat16),
            pltpu.VMEM((STEPS, n * block, PIECE), jnp.bfloat16),
            pltpu.VMEM((STEPS, n, block, 128), jnp.float32),
            pltpu.VMEM((2, block, PIECE), jnp.bfloat16),
            dma((5,)),
            dma((6,)),
            dma((STEPS, n)),
            dma((STEPS, n)),
            dma((STEPS, n)),
            dma((STEPS, n)),
            dma((STEPS,)),
            dma((STEPS,)),
            dma((STEPS, n)),
            dma((STEPS, n)),
            dma,
            dma,
        ],
        compiler_params=pltpu.CompilerParams(
            collective_id=0, has_side_effects=True, vmem_limit_bytes=63 * 1024 * 1024
        ),
        cost_estimate=pl.CostEstimate(
            flops=STEPS * 6 * n * rows * features * hid_dev,
            bytes_accessed=6 * features * hid_dev,
            transcendentals=STEPS * n * rows * hid_dev,
        ),
    )(
        hidden_states,
        draft_row,
        expert_ids,
        route_weights,
        norm_gain,
        w_gate,
        w_up,
        w_down,
    )


def by_size(mesh):
    def run(hidden_states, draft_row, expert_ids, route_weights, norm_gain, w_gate, w_up, w_down):
        ex = mesh.shape["ex"]
        rows = hidden_states.shape[0] // (ex * mesh.shape["grp"])
        every = expert_ids.shape[2] * HID == w_gate.shape[1]
        one_each = w_gate.shape[1] == ex * HID
        features = hidden_states.shape[1]
        shaped = (
            rows * QUARTERS == 16
            and features % 256 == 0
            and (QUARTERS - 1) * PIECE < features // 2 <= QUARTERS * PIECE
        )
        dense = every and one_each and shaped and mesh.shape["tp"] == 2
        in_specs = (
            P(("grp", "ex"), None),
            P(("grp", "ex")),
            P(None, ("grp", "ex"), None),
            P(None, ("grp", "ex"), None),
            P(),
            P(None, ("ex", "tp")),
            P(None, ("ex", "tp")),
            P(("ex", "tp"), None),
        )
        return jax.shard_map(
            fused_shards if dense else shards,
            mesh=mesh,
            in_specs=in_specs,
            out_specs=P(("grp", "ex"), None),
            check_vma=False,
        )(hidden_states, draft_row, expert_ids, route_weights, norm_gain, w_gate, w_up, w_down)

    return run


def solution(mesh):
    return by_size(mesh)
```
